128 devices in a mesh: rep: 4 (over z), row: 32 (over x, y, core).
Axes of the slice: x: 4, y: 4, z: 4, core: 2. Of those that a mesh axis runs over, the one named last changes fastest.
Arguments:
- basis_vecs: bfloat16 [96, 2097152], P('rep', 'row'), may hold values from -12 to 12
- potential: float32 [2097152], P('row'), may hold values from 0.3 to 3
- surface: bfloat16 [256, 256], replicated, may hold values from -0.375 to 0.375
- grid_perm: int32 [2097152], P('row'), may hold values from 0 to 65535, as said below
- kinetic: bfloat16 [256, 256], replicated, may hold values from -0.375 to 0.375
- couplings: int32 [24576, 2], P('row'), may hold values from 0 to 8191, as said below
- coupling_coefficient: float32 [24576], P('row'), may hold values from -6 to 6
- precond: float32 [32, 4, 16384], P('row', 'rep'), may hold values from 0.1 to 4
Outputs:
- new_block: float32 [96, 32, 4, 16384], P(None, 'row', 'rep')
- rayleigh: float32 [96, 96], replicated
The draws below stay inside these ranges and needn't reach their ends.
Inputs may be any that keep to these rules, and one draw needn't show every extreme that they name: `grid_perm`: each index of row holds 65536 consecutive entries forming a permutation of 0 to 65535. `couplings`: entry a 3 + m has block row a; for m = 0 the block column is a, the other 2 columns lie 1 to 2 blocks from a.
All inputs are finite; a program needn't handle non-finite values.
Results may differ from the reference program's by a relative error of at most 0.0003.
The reference program's roundings to bfloat16 on the way count: a program that leaves them out, or rounds other values in their place, can miss the bound.
Values may be sent and summed in bfloat16 or wider, within the bound.
No kernel may reach another device: no remote copies, remote signals or barrier semaphores. Data moves between devices by JAX's collectives and lax.ppermute only.
A program may use at most 192 MiB of HBM per device.

```python
import math
import jax
import jax.numpy as jnp
from jax import lax

K = 96
BSZ = 256
ROWS_DEV = 65536
HB = 2
COUPLINGS_PER_ROW = 3
NB = 2097152
QROWS = 16384
NCPL = 24576
N_REP = 4
N_ROW = 32


def draw_basis_vecs(key, part):
    key = jax.random.fold_in(key, 10)
    position = jnp.arange(NB, dtype=jnp.float32)[None, :] / NB
    values = jnp.clip(jax.random.normal(key, (K, NB), jnp.float32), -4.0, 4.0)
    amplitude = 1.0 + 2.0 * position
    return (values * amplitude).astype(jnp.bfloat16)


def draw_grid_perm(key, part):
    key = jax.random.fold_in(key, 11)
    row_keys = jax.random.split(key, NB // ROWS_DEV)
    shuffles = jax.vmap(lambda one_key: jax.random.permutation(one_key, ROWS_DEV))(row_keys)
    return shuffles.reshape(NB).astype(jnp.int32)


def draw_couplings(key, part):
    key = jax.random.fold_in(key, 12)
    total_block_count = NB // BSZ
    offsets = jnp.concatenate([jnp.arange(-HB, 0), jnp.arange(1, HB + 1)]).astype(jnp.int32)
    ranking_scores = jax.random.randint(key, (total_block_count, 2 * HB), 0, 1 << 20, dtype=jnp.int32) * (2 * HB) + jnp.arange(2 * HB, dtype=jnp.int32)
    selected_items = jnp.argsort(ranking_scores, axis=1)[:, :COUPLINGS_PER_ROW - 1]
    shifts = offsets[selected_items]
    block_rows = jnp.arange(total_block_count, dtype=jnp.int32)[:, None]
    targets = block_rows + shifts
    targets = jnp.where((targets < 0) | (targets >= total_block_count), block_rows - shifts, targets)
    target_columns = jnp.concatenate([block_rows, targets], axis=1)
    row_indices = jnp.broadcast_to(block_rows, target_columns.shape)
    return jnp.stack([row_indices, target_columns], axis=2).reshape(total_block_count * COUPLINGS_PER_ROW, 2).astype(jnp.int32)


def draw_precond(key, part):
    key = jax.random.fold_in(key, 13)
    grid_shape = (NB // ROWS_DEV, ROWS_DEV // QROWS, QROWS)
    lowest = 0.2
    climb_rate = 2.0
    base_scale = jnp.exp(jax.random.uniform(key, grid_shape, jnp.float32, jnp.log(lowest), 0.0))
    position = jnp.arange(NB, dtype=jnp.float32).reshape(grid_shape) / NB
    return base_scale * (1.0 + climb_rate * position)


def levels(key, shape, shards, least, high):
    factor_of = 1.0
    for dim, shards_of in shards:
        heights = jax.random.uniform(jax.random.fold_in(jax.random.fold_in(key, 6), dim), (shards_of,), jnp.float32, least / len(shards), high / len(shards))
        factor_of = factor_of * jnp.repeat(jnp.exp(heights), shape[dim] // shards_of).reshape((-1,) + (1,) * (len(shape) - 1 - dim))
    return factor_of


def centred(key, extent, spread, bound, cuts=(), held_as=jnp.bfloat16):
    loudness = levels(key, extent, cuts, -0.22, 0.18) if cuts else 1.0
    result = jax.random.normal(key, extent, jnp.float32) * spread * loudness
    return jnp.minimum(jnp.maximum(result, -bound), bound).astype(held_as)


def setup_inputs(seed: int = 0) -> dict:
    key_list = jax.random.split(jax.random.key(seed), 9)
    return {
        "basis_vecs": draw_basis_vecs(jax.random.fold_in(key_list[8], 71), 0),
        "potential": jnp.clip(jnp.exp(math.log(3.0) - 2.3025851 * jax.random.uniform(key_list[1], (NB,), jnp.float32) ** levels(key_list[1], (NB,), ((0, 32),), -0.2, 0.2)), 0.3, 3.0),
        "surface": centred(key_list[2], (BSZ, BSZ), BSZ ** -0.5, 0.375),
        "grid_perm": draw_grid_perm(jax.random.fold_in(key_list[8], 71), 0),
        "kinetic": centred(key_list[4], (BSZ, BSZ), BSZ ** -0.5, 0.375),
        "couplings": draw_couplings(jax.random.fold_in(key_list[8], 71), 0),
        "coupling_coefficient": centred(key_list[6], (NCPL,), 1.0, 6.0, ((0, 32),), jnp.float32),
        "precond": draw_precond(jax.random.fold_in(key_list[8], 71), 0),
    }


def potential_block(target_columns, order, pot_vals, surface):
    vec_count = target_columns.shape[0]
    picked_entries = jnp.take(target_columns, order, axis=1)
    blocks = picked_entries.reshape(vec_count, -1, BSZ).astype(jnp.float32)
    surf_wide = surface.astype(jnp.float32)
    projected = jnp.einsum('cbk,kl->cbl', blocks, surf_wide)
    weighted = (projected * pot_vals.reshape(-1, BSZ)).astype(jnp.bfloat16)
    returned = jnp.einsum('cbl,kl->cbk', weighted.astype(jnp.float32), surf_wide)
    returned = returned.astype(jnp.bfloat16).reshape(vec_count, -1)
    return jnp.zeros_like(returned).at[:, order].set(returned)

def reference(basis_vecs, potential, surface, grid_perm, kinetic, couplings, coupling_coefficient, precond):
    row_count = ROWS_DEV
    piece_rows = row_count // N_ROW
    seg_rows = piece_rows // N_REP
    total_block_count = row_count // BSZ
    grid_source = basis_vecs.reshape(K, N_ROW, N_ROW, piece_rows).transpose(2, 0, 1, 3).reshape(N_ROW, K, row_count)
    orders = grid_perm.reshape(N_ROW, row_count)
    pot_rows = potential.reshape(N_ROW, row_count)
    grid_out = lax.map(lambda packed: potential_block(packed[0], packed[1], packed[2], surface), (grid_source, orders, pot_rows))
    pot_image = grid_out.reshape(N_ROW, K, N_ROW, piece_rows).transpose(2, 1, 0, 3).reshape(N_ROW, K, row_count)
    basis_blocks = basis_vecs.reshape(K, NB // BSZ, BSZ)
    linked_rows = couplings.reshape(N_ROW, total_block_count * COUPLINGS_PER_ROW, 2)
    coefficient_values = coupling_coefficient.reshape(N_ROW, total_block_count * COUPLINGS_PER_ROW)
    bases = jnp.arange(N_ROW, dtype=jnp.int32) * total_block_count
    kin_wide = kinetic.astype(jnp.float32)

    def apply_device(packed):
        link_here, coef_here, base_block, own_pot = packed
        picked_entries = jnp.take(basis_blocks, link_here[:, 1], axis=1).astype(jnp.float32) * coef_here[None, :, None]
        summed = jax.ops.segment_sum(jnp.moveaxis(picked_entries, 1, 0), link_here[:, 0] - base_block, num_segments=total_block_count)
        source_rows = summed.astype(jnp.bfloat16)
        source_rows = lax.optimization_barrier(source_rows).astype(jnp.float32)
        kin_part = jnp.einsum('bck,kl->cbl', source_rows, kin_wide).reshape(K, row_count)
        return (kin_part + own_pot.astype(jnp.float32)).astype(jnp.bfloat16)
    image_vecs = lax.map(apply_device, (linked_rows, coefficient_values, bases, pot_image))
    highest = lax.Precision.HIGHEST

    def device_vecs(device):
        return lax.dynamic_slice_in_dim(basis_vecs, device * row_count, row_count, 1).astype(jnp.float32)

    def rayleigh_step(running, device):
        vectors = device_vecs(device)
        images = image_vecs[device].astype(jnp.float32)
        return (running + jnp.dot(vectors, images.T, precision=highest), None)
    running, _ = lax.scan(rayleigh_step, jnp.zeros((K, K), jnp.float32), jnp.arange(N_ROW, dtype=jnp.int32))
    rayleigh = running / NB
    scales = precond.reshape(N_ROW, N_REP, N_ROW, seg_rows).transpose(0, 2, 1, 3).reshape(N_ROW, row_count)

    def corrected_of(device):
        vectors = device_vecs(device)
        images = image_vecs[device].astype(jnp.float32)
        residual = images - jnp.dot(rayleigh.T, vectors, precision=highest)
        return residual * scales[device][None, :]

    def gram_step(running, device):
        corrected = corrected_of(device)
        return (running + jnp.dot(corrected, corrected.T, precision=highest), None)
    gram_total, _ = lax.scan(gram_step, jnp.zeros((K, K), jnp.float32), jnp.arange(N_ROW, dtype=jnp.int32))
    lower_factor = jnp.linalg.cholesky(gram_total / NB)

    def solve_device(device):
        return lax.linalg.triangular_solve(lower_factor, corrected_of(device), left_side=True, lower=True)
    solved = lax.map(solve_device, jnp.arange(N_ROW, dtype=jnp.int32))
    solved = solved.reshape(N_ROW, K, N_ROW, N_REP, seg_rows).transpose(1, 0, 3, 2, 4)
    new_block = solved.reshape(K, N_ROW, N_REP, QROWS)
    return (new_block, rayleigh)
```

```python
import functools

import jax
import jax.numpy as jnp
from jax import lax
from jax.experimental import pallas as pl
from jax.experimental.pallas import tpu as pltpu
from jax.sharding import PartitionSpec as P

HB = 2
COUPLINGS_PER_ROW = 3
BLK = 256
PAD = 32
GROUPS = 4
LANES = 128
SPAN = GROUPS * BLK
DEPTH = 4
VMEM_LIMIT = 60 * 2**20
NT = (((1,), (1,)), ((), ()))
WHOLE = pl.BlockSpec(memory_space=pltpu.VMEM)
SCALARS = pl.BlockSpec(memory_space=pltpu.SMEM)


def dot_nt(a, b):
    return lax.dot_general(a, b, NT, preferred_element_type=jnp.float32)


def dot_exact(a, b):
    return jnp.dot(a, b, precision=lax.Precision.HIGHEST, preferred_element_type=jnp.float32)


def iota(shape, dim):
    return lax.broadcasted_iota(jnp.int32, shape, dim)


def three_parts(x):
    high = x.astype(jnp.bfloat16)
    rest = x - high.astype(jnp.float32)
    middle = rest.astype(jnp.bfloat16)
    low = (rest - middle.astype(jnp.float32)).astype(jnp.bfloat16)
    return [high, middle, low]


def inverse_kernel(reps, perm_ref, out_ref, acc_ref):
    blocks = perm_ref.shape[0]
    acc_ref[...] = jnp.zeros_like(acc_ref)
    step = 4
    rows = iota((BLK, BLK), 0)
    lane = iota((BLK, BLK), 1).astype(jnp.float32)

    @pl.loop(0, blocks // 8)
    def _(i):
        tile = perm_ref[pl.ds(pl.multiple_of(i * 8, 8), 8), :]
        high = tile >> 8
        low = tile & 255
        for part in range(8 // step):
            left, right = [], []
            for k in range(step):
                at = part * step + k
                hit = rows == high[at:at + 1, :]
                number = (i * 8 + at).astype(jnp.float32)
                left.append(jnp.concatenate(
                    [jnp.where(hit, number, 0.0), jnp.where(hit, lane, 0.0)], axis=0
                ).astype(jnp.bfloat16))
                right.append(jnp.where(rows == low[at:at + 1, :], 1.0, 0.0).astype(jnp.bfloat16))
            acc_ref[...] += dot_nt(jnp.concatenate(left, axis=1), jnp.concatenate(right, axis=1))

    per_rep = 8 // reps
    for d in range(blocks // 8):
        tile = acc_ref[d * 8:(d + 1) * 8, :] * 256.0 + acc_ref[BLK + d * 8:BLK + (d + 1) * 8, :]
        tile = tile.astype(jnp.int32)
        for b in range(reps):
            start = b * (blocks // reps) + d * per_rep
            out_ref[start:start + per_rep, :] = tile[b * per_rep:(b + 1) * per_rep, :]


def inverse_of(perm, reps):
    blocks = perm.shape[0] // BLK
    return pl.pallas_call(
        functools.partial(inverse_kernel, reps),
        out_shape=jax.ShapeDtypeStruct((blocks, BLK), jnp.int32),
        in_specs=[WHOLE],
        out_specs=WHOLE,
        scratch_shapes=[pltpu.VMEM((2 * BLK, BLK), jnp.float32)],
        compiler_params=pltpu.CompilerParams(vmem_limit_bytes=VMEM_LIMIT),
        cost_estimate=pl.CostEstimate(
            flops=4 * BLK * BLK * blocks * BLK, bytes_accessed=8 * blocks * BLK, transcendentals=0
        ),
    )(perm.reshape(blocks, BLK)).reshape(-1)


def stream(index_ref, count, slots, sems, table_ref, rows_refs, work):
    sublane = iota((8, LANES), 0)

    def fetch(i, slot):
        start = pl.multiple_of(jnp.minimum(i, count - 1) * SPAN, SPAN)
        return pltpu.make_async_copy(index_ref.at[pl.ds(start, SPAN)], slots[slot], sems.at[slot])

    def gather(slot, rows_ref):
        def tile(first):
            value = None
            for t in range(8):
                at = slots[slot][first + t]
                row = jnp.broadcast_to(table_ref[pl.ds(at, 1), :], (8, LANES))
                value = row if value is None else jnp.where(sublane == t, row, value)
            return value

        for first in range(0, SPAN, 16):
            both = jnp.concatenate([tile(first), tile(first + 8)], axis=0)
            rows_ref[first:first + 16, :] = both.astype(jnp.bfloat16)

    def begin():
        for slot in range(DEPTH):
            fetch(slot, slot).start()

    def run():
        fetch(0, 0).wait()
        gather(0, rows_refs[0])
        fetch(DEPTH, 0).start()

        @pl.loop(0, count // DEPTH)
        def _(j):
            for s in range(DEPTH):
                i = j * DEPTH + s
                slot = (s + 1) % DEPTH
                fetch(i + 1, slot).wait()
                gather(slot, rows_refs[(s + 1) % 2])
                work(i, rows_refs[s % 2])
                fetch(i + 1 + DEPTH, slot).start()

        for slot in range(DEPTH):
            fetch(count, slot).wait()

    return begin, run


def surface_kernel(
    x_ref, perm_ref, back_ref, pot_ref, surf_ref, out_ref,
    table_ref, packed_ref, even_ref, odd_ref, *rest
):
    slots, sems = rest[:-1], rest[-1]
    pieces, vecs, width = x_ref.shape
    points = table_ref.shape[0]
    per_group = pieces // GROUPS
    group_rows = points // GROUPS
    row, column = iota((LANES, GROUPS * LANES), 0), iota((LANES, GROUPS * LANES), 1)
    fold = jnp.where(
        (row // PAD == column // LANES) & (row % PAD == column % PAD), 1.0, 0.0
    ).astype(jnp.bfloat16)
    unit = jnp.where(iota((BLK, BLK), 0) == iota((BLK, BLK), 1), 1.0, 0.0).astype(jnp.bfloat16)
    lane_group = iota((BLK, LANES), 1) // PAD
    count = points // SPAN

    def folded(rows_ref):
        wide = jnp.concatenate([rows_ref[q * BLK:(q + 1) * BLK, :] for q in range(GROUPS)], axis=1)
        return dot_nt(fold, wide)

    def spread(rows, starts):
        for q in range(GROUPS):
            table_ref[pl.ds(pl.multiple_of(starts[q], BLK), BLK), :] = jnp.where(
                lane_group == q, rows, 0.0
            )

    def to_grid_and_back(i, rows_ref):
        values = folded(rows_ref).astype(jnp.bfloat16)
        projected = jnp.dot(values, surf_ref[...], preferred_element_type=jnp.float32)
        weighted = jnp.concatenate([
            projected[q * PAD:(q + 1) * PAD] * pot_ref[pl.ds(i * GROUPS + q, 1), :]
            for q in range(GROUPS)
        ], axis=0).astype(jnp.bfloat16)
        returned = dot_nt(surf_ref[...], weighted).astype(jnp.bfloat16).astype(jnp.float32)
        packed_ref[pl.ds(pl.multiple_of(i * BLK, BLK), BLK), :] = returned

    def to_basis(i, rows_ref):
        values = folded(rows_ref).astype(jnp.bfloat16)
        per_piece = out_ref.shape[2] // BLK
        for q in range(GROUPS):
            at = (q % per_piece) * BLK
            out_ref[i * (GROUPS // per_piece) + q // per_piece, :, at:at + BLK] = values[
                q * PAD:q * PAD + vecs
            ]

    begin, run = stream(perm_ref, count, slots, sems, table_ref, (even_ref, odd_ref), to_grid_and_back)
    begin()
    chunk = 512

    @pl.loop(0, per_group)
    def _(d):
        for c in range(0, width, chunk):
            parts = []
            for q in range(GROUPS):
                parts.append(x_ref[q * per_group + d, :, c:c + chunk].astype(jnp.float32))
                parts.append(jnp.zeros((PAD - vecs, chunk), jnp.float32))
            stacked = jnp.concatenate(parts, axis=0).astype(jnp.bfloat16)
            for h in range(0, chunk, BLK):
                rows = dot_nt(unit, stacked[:, h:h + BLK])
                spread(rows, [q * group_rows + d * width + c + h for q in range(GROUPS)])

    run()
    begin, run = stream(back_ref, count, slots, sems, table_ref, (even_ref, odd_ref), to_basis)
    begin()

    @pl.loop(0, count)
    def _(i):
        rows = packed_ref[pl.ds(pl.multiple_of(i * BLK, BLK), BLK), :]
        spread(rows, [i * SPAN + q * BLK for q in range(GROUPS)])

    run()


def surface_pass(arrived, perm, back, potential, surface, reps):
    pieces, vecs, width = arrived.shape
    points = perm.shape[0]
    return pl.pallas_call(
        surface_kernel,
        out_shape=jax.ShapeDtypeStruct((pieces * reps, vecs, width // reps), jnp.bfloat16),
        in_specs=[WHOLE] * 5,
        out_specs=WHOLE,
        scratch_shapes=[
            pltpu.VMEM((points, LANES), jnp.float32),
            pltpu.VMEM((points // GROUPS, LANES), jnp.float32),
            pltpu.VMEM((SPAN, LANES), jnp.bfloat16),
            pltpu.VMEM((SPAN, LANES), jnp.bfloat16),
        ] + [pltpu.SMEM((SPAN,), jnp.int32)] * DEPTH + [pltpu.SemaphoreType.DMA((DEPTH,))],
        compiler_params=pltpu.CompilerParams(vmem_limit_bytes=VMEM_LIMIT),
        cost_estimate=pl.CostEstimate(
            flops=4 * vecs * points * BLK, bytes_accessed=300_000_000, transcendentals=0
        ),
    )(arrived, perm, back, potential.reshape(-1, BLK), surface)


def source_kernel(vecs_ref, low_ref, high_ref, column_ref, weight_ref, out_ref, wide_ref):
    reps = out_ref.shape[0]
    edge = low_ref.shape[1]
    rows = vecs_ref.shape[1]
    blocks = rows // BLK
    piece_blocks = out_ref.shape[3] * reps // (blocks * BLK)
    wide_ref[:, 0:edge] = low_ref[...]
    wide_ref[:, edge + rows:] = high_ref[...]
    per_piece = 8
    per_rep = per_piece // reps

    @pl.loop(0, blocks // per_piece)
    def _(j):
        start = pl.multiple_of(j * per_piece * BLK, per_piece * BLK)
        wide_ref[:, pl.ds(edge + start, per_piece * BLK)] = vecs_ref[:, pl.ds(start, per_piece * BLK)]

    @pl.loop(0, blocks // per_piece)
    def _(j):
        for k in range(per_piece):
            a = j * per_piece + k
            total = None
            for m in range(COUPLINGS_PER_ROW):
                c = a * COUPLINGS_PER_ROW + m
                at = pl.multiple_of(column_ref[c] * BLK, BLK)
                term = wide_ref[:, pl.ds(at, BLK)].astype(jnp.float32) * weight_ref[c]
                total = term if total is None else total + term
            to = pl.ds(pl.multiple_of(j * per_rep * BLK, per_rep * BLK) + (k % per_rep) * BLK, BLK)
            here = pl.multiple_of(a * BLK, BLK)
            out_ref[k // per_rep, 0, :, to] = vecs_ref[:, pl.ds(here, BLK)]
            out_ref[k // per_rep, 1, :, to] = total.astype(jnp.bfloat16)


def source_of(basis_vecs, low, high, columns, weights, reps):
    vecs, rows = basis_vecs.shape
    return pl.pallas_call(
        source_kernel,
        out_shape=jax.ShapeDtypeStruct((reps, 2, vecs, rows // reps), jnp.bfloat16),
        in_specs=[WHOLE, WHOLE, WHOLE, SCALARS, SCALARS],
        out_specs=WHOLE,
        scratch_shapes=[pltpu.VMEM((vecs, rows + 2 * low.shape[1]), jnp.bfloat16)],
        compiler_params=pltpu.CompilerParams(vmem_limit_bytes=VMEM_LIMIT),
        cost_estimate=pl.CostEstimate(
            flops=6 * vecs * rows, bytes_accessed=12 * vecs * rows, transcendentals=0
        ),
    )(basis_vecs, low, high, columns, weights)


def image_kernel(moved_ref, pot_ref, kinetic_ref, precond_ref, image_ref, sums_ref, left_ref, right_ref):
    step = pl.program_id(0)
    reps, _, vecs, width = moved_ref.shape
    segment = pot_ref.shape[3]
    count = reps * vecs

    @pl.when(step == 0)
    def _():
        left_ref[...] = jnp.zeros_like(left_ref)
        right_ref[...] = jnp.zeros_like(right_ref)

    for s in range(width // segment):
        at = slice(s * segment, (s + 1) * segment)

        def joined(k):
            parts = [moved_ref[b, k, :, at].astype(jnp.float32) for b in range(reps)]
            return jnp.concatenate(parts, axis=0)

        vectors = joined(0)
        source = joined(1).astype(jnp.bfloat16)
        kin = jnp.concatenate([
            jnp.dot(source[:, h:h + BLK], kinetic_ref[...], preferred_element_type=jnp.float32)
            for h in range(0, segment, BLK)
        ], axis=1)
        pot = jnp.concatenate([pot_ref[b, s].astype(jnp.float32) for b in range(reps)], axis=0)
        image = (kin + pot).astype(jnp.bfloat16)
        image_ref[:, at] = image
        scale = precond_ref[0:1, at]
        square = scale * scale
        vectors_16 = vectors.astype(jnp.bfloat16)
        both = jnp.concatenate([image, vectors_16], axis=0)
        image_parts = three_parts(image.astype(jnp.float32) * square)
        vector_parts = three_parts(vectors * square)
        left_ref[...] += dot_nt(jnp.concatenate(image_parts, axis=0), both)
        right_ref[...] += dot_nt(jnp.concatenate([vectors_16] + vector_parts, axis=0), both)

    @pl.when(step == pl.num_programs(0) - 1)
    def _():
        left = left_ref[0:count] + left_ref[count:2 * count] + left_ref[2 * count:3 * count]
        right = (
            right_ref[count:2 * count] + right_ref[2 * count:3 * count] + right_ref[3 * count:4 * count]
        )
        sums_ref[0] = right_ref[0:count, 0:count]
        sums_ref[1] = left[:, 0:count]
        sums_ref[2] = left[:, count:2 * count]
        sums_ref[3] = right[:, count:2 * count]


def image_of(moved, pot, kinetic, precond, steps):
    reps, _, vecs, rows = moved.shape
    width = rows // steps
    count = reps * vecs
    pieces = pot.shape[1] // steps
    return pl.pallas_call(
        image_kernel,
        grid=(steps,),
        out_shape=(
            jax.ShapeDtypeStruct((count, rows), jnp.bfloat16),
            jax.ShapeDtypeStruct((4, count, count), jnp.float32),
        ),
        in_specs=[
            pl.BlockSpec((reps, 2, vecs, width), lambda i: (0, 0, 0, i)),
            pl.BlockSpec((reps, pieces, vecs, pot.shape[3]), lambda i: (0, i, 0, 0)),
            pl.BlockSpec((BLK, BLK), lambda i: (0, 0)),
            pl.BlockSpec((1, width), lambda i: (0, i)),
        ],
        out_specs=(
            pl.BlockSpec((count, width), lambda i: (0, i)),
            pl.BlockSpec((4, count, count), lambda i: (0, 0, 0)),
        ),
        scratch_shapes=[
            pltpu.VMEM((3 * count, 2 * count), jnp.float32),
            pltpu.VMEM((4 * count, 2 * count), jnp.float32),
        ],
        compiler_params=pltpu.CompilerParams(vmem_limit_bytes=VMEM_LIMIT),
        cost_estimate=pl.CostEstimate(
            flops=28 * count * count * rows, bytes_accessed=8 * count * rows, transcendentals=0
        ),
    )(moved, pot, kinetic, precond)


def solve_kernel(full_rows, sums_ref, moved_ref, image_ref, precond_ref, out_ref, rayleigh_ref, mix_ref):
    count = image_ref.shape[0]
    reps, _, vecs, width = moved_ref.shape

    @pl.when(pl.program_id(0) == 0)
    def _():
        rayleigh = sums_ref[0] / full_rows
        rayleigh_ref[...] = rayleigh
        turned = rayleigh.T
        cross = dot_exact(sums_ref[2], rayleigh)
        last = dot_exact(turned, dot_exact(sums_ref[3], rayleigh))
        gram = (sums_ref[1] - cross - cross.T + last) / full_rows
        pad = jnp.zeros((count, LANES - count), jnp.float32)
        row, column = iota((count, LANES), 0), iota((count, LANES), 1)
        left = jnp.concatenate([gram, pad], axis=1)
        right = jnp.where(row == column, 1.0, 0.0)
        for j in range(count):
            pivot_left, pivot_right = left[j:j + 1, :], right[j:j + 1, :]
            ratio = left[:, j:j + 1] / pivot_left[:, j:j + 1]
            ratio = jnp.where(row[:, 0:1] > j, ratio, 0.0)
            left = left - ratio * pivot_left
            right = right - ratio * pivot_right
        diagonal = jnp.sum(jnp.where(row == column, left, 0.0), axis=1, keepdims=True)
        inverse = (right * lax.rsqrt(diagonal))[:, 0:count]
        parts = three_parts(inverse) + three_parts(-dot_exact(inverse, turned))
        for k in range(3):
            mix_ref[k * count:(k + 1) * count, 0:count] = parts[k]
            mix_ref[k * count:(k + 1) * count, count:2 * count] = parts[3 + k]

    vectors = jnp.concatenate(
        [moved_ref[b, 0].astype(jnp.float32) for b in range(reps)], axis=0
    ).astype(jnp.bfloat16)
    both = jnp.concatenate([image_ref[...], vectors], axis=0)
    chunk = 512
    for s in range(0, width, chunk):
        parts = jnp.dot(mix_ref[...], both[:, s:s + chunk], preferred_element_type=jnp.float32)
        total = (parts[2 * count:] + parts[count:2 * count]) + parts[0:count]
        out_ref[:, s:s + chunk] = total * precond_ref[0:1, s:s + chunk]


def solved_of(sums, moved, image, precond, full_rows, steps):
    reps, _, vecs, rows = moved.shape
    width = rows // steps
    count = reps * vecs
    return pl.pallas_call(
        functools.partial(solve_kernel, full_rows),
        grid=(steps,),
        out_shape=(
            jax.ShapeDtypeStruct((count, rows), jnp.float32),
            jax.ShapeDtypeStruct((count, count), jnp.float32),
        ),
        in_specs=[
            pl.BlockSpec((4, count, count), lambda i: (0, 0, 0)),
            pl.BlockSpec((reps, 1, vecs, width), lambda i: (0, 0, 0, i)),
            pl.BlockSpec((count, width), lambda i: (0, i)),
            pl.BlockSpec((1, width), lambda i: (0, i)),
        ],
        out_specs=(
            pl.BlockSpec((count, width), lambda i: (0, i)),
            pl.BlockSpec((count, count), lambda i: (0, 0)),
        ),
        scratch_shapes=[pltpu.VMEM((3 * count, 2 * count), jnp.bfloat16)],
        compiler_params=pltpu.CompilerParams(vmem_limit_bytes=VMEM_LIMIT),
        cost_estimate=pl.CostEstimate(
            flops=12 * count * count * rows, bytes_accessed=8 * count * rows, transcendentals=0
        ),
    )(sums, moved, image, precond)


def sum_over_devices(x):
    def turned(axis, stride, shift):
        size = lax.axis_size(axis)
        pairs = []
        for i in range(size):
            digit = (i // stride) % 4
            pairs.append((i, i + ((digit + shift) % 4 - digit) * stride))
        return lax.ppermute(x, axis, pairs)

    x = x + lax.ppermute(x, "row", [(i, i ^ 1) for i in range(lax.axis_size("row"))])
    for axis, stride in (("rep", 1), ("row", 8), ("row", 2)):
        up, down, across = (turned(axis, stride, shift) for shift in (1, 3, 2))
        x = (x + across) + (up + down)
    return x


def body(
    basis_vecs, potential, surface, grid_perm, kinetic, couplings, coupling_coefficient, precond
):
    vecs, rows = basis_vecs.shape
    pieces = lax.axis_size("row")
    reps = lax.axis_size("rep")
    width = rows // pieces
    blocks = rows // BLK
    edge = HB * BLK
    forward = [(i, i + 1) for i in range(pieces - 1)]
    backward = [(i + 1, i) for i in range(pieces - 1)]
    low = lax.ppermute(basis_vecs[:, rows - edge:], "row", forward)
    high = lax.ppermute(basis_vecs[:, :edge], "row", backward)
    by_piece = basis_vecs.reshape(vecs, pieces, width).transpose(1, 0, 2)
    arrived = lax.all_to_all(by_piece, "row", split_axis=0, concat_axis=0, tiled=True)
    columns = couplings[:, 1] - (lax.axis_index("row") * blocks - HB)
    by_rep = source_of(basis_vecs, low, high, columns, coupling_coefficient, reps)
    moved = lax.all_to_all(by_rep, "rep", split_axis=0, concat_axis=0, tiled=True)
    back = inverse_of(grid_perm, reps)
    restored = surface_pass(arrived, grid_perm, back, potential, surface, reps)
    pot = lax.all_to_all(restored, ("rep", "row"), split_axis=0, concat_axis=0, tiled=True)
    pot = pot.reshape(reps, pieces, vecs, width // reps)
    scale = precond.reshape(1, -1)
    image, sums = image_of(moved, pot, kinetic, scale, 8)
    count = reps * vecs
    sums = sum_over_devices(sums.reshape(4 * count, count)).reshape(4, count, count)
    solved, rayleigh = solved_of(sums, moved, image, scale, float(rows * pieces), 8)
    return (solved.reshape(count, 1, 1, -1), rayleigh)


def solution(mesh):
    in_specs = (
        P("rep", "row"),
        P("row"),
        P(),
        P("row"),
        P(),
        P("row", None),
        P("row"),
        P("row", "rep", None),
    )
    out_specs = (P(None, "row", "rep", None), P())
    return jax.shard_map(body, mesh=mesh, in_specs=in_specs, out_specs=out_specs, check_vma=False)
```

```python
import functools

import jax
import jax.numpy as jnp
from jax import lax
from jax.experimental import pallas as pl
from jax.experimental.pallas import tpu as pltpu
from jax.sharding import PartitionSpec as P

HB = 2
COUPLINGS_PER_ROW = 3
BLK = 256
PAD = 32
GROUPS = 4
LANES = 128
SPAN = GROUPS * BLK
VMEM_LIMIT = 60 * 2**20
NT = (((1,), (1,)), ((), ()))
WHOLE = pl.BlockSpec(memory_space=pltpu.VMEM)
SCALARS = pl.BlockSpec(memory_space=pltpu.SMEM)


def dot_nt(a, b):
    return lax.dot_general(a, b, NT, preferred_element_type=jnp.float32)


def dot_exact(a, b):
    return jnp.dot(a, b, precision=lax.Precision.HIGHEST, preferred_element_type=jnp.float32)


def iota(shape, dim):
    return lax.broadcasted_iota(jnp.int32, shape, dim)


def three_parts(x):
    high = x.astype(jnp.bfloat16)
    rest = x - high.astype(jnp.float32)
    middle = rest.astype(jnp.bfloat16)
    low = (rest - middle.astype(jnp.float32)).astype(jnp.bfloat16)
    return [high, middle, low]


def inverse_kernel(reps, perm_ref, out_ref, back_ref, acc_ref):
    blocks = perm_ref.shape[0]
    acc_ref[...] = jnp.zeros_like(acc_ref)
    step = 4
    rows = iota((BLK, BLK), 0)
    lane = iota((BLK, BLK), 1).astype(jnp.float32)

    @pl.loop(0, blocks // 8)
    def _(i):
        tile = perm_ref[pl.ds(pl.multiple_of(i * 8, 8), 8), :]
        high = tile >> 8
        low = tile & 255
        for part in range(8 // step):
            left, right = [], []
            for k in range(step):
                at = part * step + k
                hit = rows == high[at:at + 1, :]
                number = (i * 8 + at).astype(jnp.float32)
                left.append(jnp.concatenate(
                    [jnp.where(hit, number, 0.0), jnp.where(hit, lane, 0.0)], axis=0
                ).astype(jnp.bfloat16))
                right.append(jnp.where(rows == low[at:at + 1, :], 1.0, 0.0).astype(jnp.bfloat16))
            acc_ref[...] += dot_nt(jnp.concatenate(left, axis=1), jnp.concatenate(right, axis=1))

    acc_ref[0:BLK, :] = acc_ref[0:BLK, :] * 256.0 + acc_ref[BLK:2 * BLK, :]
    per_rep = 8 // reps
    for d in range(blocks // 8):
        tile = acc_ref[d * 8:(d + 1) * 8, :]
        for b in range(reps):
            start = BLK + b * (blocks // reps) + d * per_rep
            acc_ref[start:start + per_rep, :] = tile[b * per_rep:(b + 1) * per_rep, :]
    half = blocks // 2
    for k in range(2):
        out_ref[k * BLK:(k + 1) * BLK, :] = perm_ref[k * half:(k + 1) * half, :].T
        back_ref[k * BLK:(k + 1) * BLK, :] = acc_ref[
            BLK + k * half:BLK + (k + 1) * half, :
        ].T.astype(jnp.int32)


def index_streams(perm, reps):
    blocks = perm.shape[0] // BLK
    streams = jax.ShapeDtypeStruct((2 * BLK, blocks // 2), jnp.int32)
    out, back = pl.pallas_call(
        functools.partial(inverse_kernel, reps),
        out_shape=(streams, streams),
        in_specs=[WHOLE],
        out_specs=(WHOLE, WHOLE),
        scratch_shapes=[pltpu.VMEM((2 * BLK, BLK), jnp.float32)],
        compiler_params=pltpu.CompilerParams(vmem_limit_bytes=VMEM_LIMIT),
        cost_estimate=pl.CostEstimate(
            flops=4 * BLK * BLK * blocks * BLK, bytes_accessed=8 * blocks * BLK, transcendentals=0
        ),
    )(perm.reshape(blocks, BLK))
    return out.reshape(-1), back.reshape(-1)


def stream(index_ref, streams, sem, table_ref, rows_refs, work):
    sublane = iota((8, LANES), 0)
    size = streams[0].shape[0]
    half = size // 8
    count = half // 2
    copies = [
        pltpu.make_async_copy(index_ref.at[pl.ds(k * size, size)], held, sem.at[k])
        for k, held in enumerate(streams)
    ]

    def gather(i, rows_ref):
        def tile(held, places):
            value = None
            for t in range(8):
                row = jnp.broadcast_to(table_ref[pl.ds(held[places[t]], 1), :], (8, LANES))
                value = row if value is None else jnp.where(sublane == t, row, value)
            return value

        for part in range(2):
            places = [t * half + 2 * i + part for t in range(8)]
            for k in range(0, len(streams), 2):
                both = jnp.concatenate([tile(held, places) for held in streams[k:k + 2]], axis=0)
                first = part * len(streams) * 8 + k * 8
                rows_ref[first:first + 16, :] = both.astype(jnp.bfloat16)

    def begin():
        for copy in copies:
            copy.start()

    def run():
        for copy in copies:
            copy.wait()
        gather(0, rows_refs[0])

        @pl.loop(0, count // 2)
        def _(j):
            for s in range(2):
                i = j * 2 + s
                gather(jnp.minimum(i + 1, count - 1), rows_refs[(s + 1) % 2])
                work(i, rows_refs[s % 2])

    return begin, run


def blocks_of(i, blocks):
    return [2 * i, 2 * i + blocks // 2, 2 * i + 1, 2 * i + 1 + blocks // 2]


def surface_kernel(
    x_ref, perm_ref, back_ref, pot_ref, surf_ref, out_ref,
    table_ref, packed_ref, even_ref, odd_ref, *rest
):
    streams, sem = rest[:-1], rest[-1]
    pieces, vecs, width = x_ref.shape
    points = table_ref.shape[0]
    per_group = pieces // GROUPS
    group_rows = points // GROUPS
    row, column = iota((LANES, GROUPS * LANES), 0), iota((LANES, GROUPS * LANES), 1)
    fold = jnp.where(
        (row // PAD == column // LANES) & (row % PAD == column % PAD), 1.0, 0.0
    ).astype(jnp.bfloat16)
    unit = jnp.where(iota((BLK, BLK), 0) == iota((BLK, BLK), 1), 1.0, 0.0).astype(jnp.bfloat16)
    lane_group = iota((BLK, LANES), 1) // PAD
    count = points // SPAN
    blocks = points // BLK

    def folded(rows_ref):
        wide = jnp.concatenate([rows_ref[q * BLK:(q + 1) * BLK, :] for q in range(GROUPS)], axis=1)
        return dot_nt(fold, wide)

    def spread(rows, starts):
        for q in range(GROUPS):
            table_ref[pl.ds(pl.multiple_of(starts[q], BLK), BLK), :] = jnp.where(
                lane_group == q, rows, 0.0
            )

    def to_grid_and_back(i, rows_ref):
        values = folded(rows_ref).astype(jnp.bfloat16)
        projected = jnp.dot(values, surf_ref[...], preferred_element_type=jnp.float32)
        weighted = jnp.concatenate([
            projected[q * PAD:(q + 1) * PAD] * pot_ref[pl.ds(block, 1), :]
            for q, block in enumerate(blocks_of(i, blocks))
        ], axis=0).astype(jnp.bfloat16)
        returned = dot_nt(surf_ref[...], weighted).astype(jnp.bfloat16).astype(jnp.float32)
        packed_ref[pl.ds(pl.multiple_of(i * BLK, BLK), BLK), :] = returned

    def to_basis(i, rows_ref):
        values = folded(rows_ref).astype(jnp.bfloat16)
        per_piece = out_ref.shape[2] // BLK
        for q in range(GROUPS):
            at = (q // per_piece) * BLK
            out_ref[i + (q % per_piece) * (out_ref.shape[0] // per_piece), :, at:at + BLK] = values[
                q * PAD:q * PAD + vecs
            ]

    begin, run = stream(perm_ref, streams, sem, table_ref, (even_ref, odd_ref), to_grid_and_back)
    begin()
    chunk = 512

    @pl.loop(0, per_group)
    def _(d):
        for c in range(0, width, chunk):
            parts = []
            for q in range(GROUPS):
                parts.append(x_ref[q * per_group + d, :, c:c + chunk].astype(jnp.float32))
                parts.append(jnp.zeros((PAD - vecs, chunk), jnp.float32))
            stacked = jnp.concatenate(parts, axis=0).astype(jnp.bfloat16)
            for h in range(0, chunk, BLK):
                rows = dot_nt(unit, stacked[:, h:h + BLK])
                spread(rows, [q * group_rows + d * width + c + h for q in range(GROUPS)])

    run()
    begin, run = stream(back_ref, streams, sem, table_ref, (even_ref, odd_ref), to_basis)
    begin()

    @pl.loop(0, count)
    def _(i):
        rows = packed_ref[pl.ds(pl.multiple_of(i * BLK, BLK), BLK), :]
        spread(rows, [block * BLK for block in blocks_of(i, blocks)])

    run()


def surface_pass(arrived, perm, back, potential, surface, reps):
    pieces, vecs, width = arrived.shape
    points = perm.shape[0]
    return pl.pallas_call(
        surface_kernel,
        out_shape=jax.ShapeDtypeStruct((pieces * reps, vecs, width // reps), jnp.bfloat16),
        in_specs=[WHOLE] * 5,
        out_specs=WHOLE,
        scratch_shapes=[
            pltpu.VMEM((points, LANES), jnp.float32),
            pltpu.VMEM((points // GROUPS, LANES), jnp.float32),
            pltpu.VMEM((SPAN, LANES), jnp.bfloat16),
            pltpu.VMEM((SPAN, LANES), jnp.bfloat16),
        ] + [pltpu.SMEM((4 * BLK,), jnp.int32)] * 64 + [pltpu.SemaphoreType.DMA((64,))],
        compiler_params=pltpu.CompilerParams(vmem_limit_bytes=VMEM_LIMIT),
        cost_estimate=pl.CostEstimate(
            flops=4 * vecs * points * BLK, bytes_accessed=300_000_000, transcendentals=0
        ),
    )(arrived, perm, back, potential.reshape(-1, BLK), surface)


def source_kernel(vecs_ref, low_ref, high_ref, column_ref, weight_ref, out_ref, wide_ref):
    reps = out_ref.shape[0]
    edge = low_ref.shape[1]
    rows = vecs_ref.shape[1]
    blocks = rows // BLK
    piece_blocks = out_ref.shape[3] * reps // (blocks * BLK)
    wide_ref[:, 0:edge] = low_ref[...]
    wide_ref[:, edge + rows:] = high_ref[...]
    per_piece = 8
    per_rep = per_piece // reps

    @pl.loop(0, blocks // per_piece)
    def _(j):
        start = pl.multiple_of(j * per_piece * BLK, per_piece * BLK)
        wide_ref[:, pl.ds(edge + start, per_piece * BLK)] = vecs_ref[:, pl.ds(start, per_piece * BLK)]

    @pl.loop(0, blocks // per_piece)
    def _(j):
        for k in range(per_piece):
            a = j * per_piece + k
            total = None
            for m in range(COUPLINGS_PER_ROW):
                c = a * COUPLINGS_PER_ROW + m
                at = pl.multiple_of(column_ref[c] * BLK, BLK)
                term = wide_ref[:, pl.ds(at, BLK)].astype(jnp.float32) * weight_ref[c]
                total = term if total is None else total + term
            to = pl.ds(pl.multiple_of(j * per_rep * BLK, per_rep * BLK) + (k % per_rep) * BLK, BLK)
            here = pl.multiple_of(a * BLK, BLK)
            out_ref[k // per_rep, 0, :, to] = vecs_ref[:, pl.ds(here, BLK)]
            out_ref[k // per_rep, 1, :, to] = total.astype(jnp.bfloat16)


def source_of(basis_vecs, low, high, columns, weights, reps):
    vecs, rows = basis_vecs.shape
    return pl.pallas_call(
        source_kernel,
        out_shape=jax.ShapeDtypeStruct((reps, 2, vecs, rows // reps), jnp.bfloat16),
        in_specs=[WHOLE, WHOLE, WHOLE, SCALARS, SCALARS],
        out_specs=WHOLE,
        scratch_shapes=[pltpu.VMEM((vecs, rows + 2 * low.shape[1]), jnp.bfloat16)],
        compiler_params=pltpu.CompilerParams(vmem_limit_bytes=VMEM_LIMIT),
        cost_estimate=pl.CostEstimate(
            flops=6 * vecs * rows, bytes_accessed=12 * vecs * rows, transcendentals=0
        ),
    )(basis_vecs, low, high, columns, weights)


def vector_kernel(moved_ref, precond_ref, sums_ref, total_ref):
    step = pl.program_id(0)
    reps, _, vecs, width = moved_ref.shape
    count = reps * vecs

    @pl.when(step == 0)
    def _():
        total_ref[...] = jnp.zeros_like(total_ref)

    for s in range(0, width, 512):
        at = slice(s, s + 512)
        parts = [moved_ref[b, 0, :, at].astype(jnp.float32) for b in range(reps)]
        vectors = jnp.concatenate(parts, axis=0)
        scale = precond_ref[0:1, at]
        left = jnp.concatenate(three_parts(vectors * (scale * scale)), axis=0)
        total_ref[...] += dot_nt(left, vectors.astype(jnp.bfloat16))

    @pl.when(step == pl.num_programs(0) - 1)
    def _():
        sums_ref[...] = (
            total_ref[0:count] + total_ref[count:2 * count] + total_ref[2 * count:3 * count]
        )


def vector_sums(moved, precond, steps):
    reps, _, vecs, rows = moved.shape
    width = rows // steps
    count = reps * vecs
    return pl.pallas_call(
        vector_kernel,
        grid=(steps,),
        out_shape=jax.ShapeDtypeStruct((count, count), jnp.float32),
        in_specs=[
            pl.BlockSpec((reps, 1, vecs, width), lambda i: (0, 0, 0, i)),
            pl.BlockSpec((1, width), lambda i: (0, i)),
        ],
        out_specs=pl.BlockSpec((count, count), lambda i: (0, 0)),
        scratch_shapes=[pltpu.VMEM((3 * count, count), jnp.float32)],
        compiler_params=pltpu.CompilerParams(vmem_limit_bytes=VMEM_LIMIT),
        cost_estimate=pl.CostEstimate(
            flops=6 * count * count * rows, bytes_accessed=2 * count * rows, transcendentals=0
        ),
    )(moved, precond)


def image_kernel(moved_ref, pot_ref, kinetic_ref, precond_ref, image_ref, sums_ref, total_ref):
    step = pl.program_id(0)
    reps, _, vecs, width = moved_ref.shape
    segment = pot_ref.shape[3]
    count = reps * vecs

    @pl.when(step == 0)
    def _():
        total_ref[...] = jnp.zeros_like(total_ref)

    def joined(k, at):
        parts = [moved_ref[b, k, :, at].astype(jnp.float32) for b in range(reps)]
        return jnp.concatenate(parts, axis=0).astype(jnp.bfloat16)

    source = joined(1, slice(0, width))
    blocks = [source[:, h:h + BLK] for h in range(0, width, BLK)]
    kin_blocks = jnp.dot(
        jnp.concatenate(blocks, axis=0), kinetic_ref[...], preferred_element_type=jnp.float32
    )
    per_segment = segment // BLK

    for s in range(width // segment):
        at = slice(s * segment, (s + 1) * segment)
        vectors = joined(0, at)
        kin = jnp.concatenate([
            kin_blocks[h * count:(h + 1) * count]
            for h in range(s * per_segment, (s + 1) * per_segment)
        ], axis=1)
        pot = jnp.concatenate([pot_ref[b, s].astype(jnp.float32) for b in range(reps)], axis=0)
        image = (kin + pot).astype(jnp.bfloat16)
        image_ref[:, at] = image
        scale = precond_ref[0:1, at]
        scaled = three_parts(image.astype(jnp.float32) * (scale * scale))
        left = jnp.concatenate(scaled + [image], axis=0)
        total_ref[...] += dot_nt(left, jnp.concatenate([image, vectors], axis=0))

    @pl.when(step == pl.num_programs(0) - 1)
    def _():
        scaled = total_ref[0:count] + total_ref[count:2 * count] + total_ref[2 * count:3 * count]
        own, cross = scaled[:, 0:count], scaled[:, count:2 * count]
        plain = total_ref[3 * count:4 * count, count:2 * count]
        sums_ref[0:count, :] = jnp.concatenate([own, cross[:, 0:PAD]], axis=1)
        sums_ref[count:2 * count, :] = jnp.concatenate([plain, cross[:, PAD:2 * PAD]], axis=1)
        sums_ref[2 * count:, :] = jnp.concatenate(
            [cross[b * vecs:(b + 1) * vecs, 2 * PAD:3 * PAD] for b in range(reps)], axis=1
        )


def image_of(moved, pot, kinetic, precond, steps):
    reps, _, vecs, rows = moved.shape
    width = rows // steps
    count = reps * vecs
    pieces = pot.shape[1] // steps
    packed = (2 * count + vecs, LANES)
    return pl.pallas_call(
        image_kernel,
        grid=(steps,),
        out_shape=(
            jax.ShapeDtypeStruct((count, rows), jnp.bfloat16),
            jax.ShapeDtypeStruct(packed, jnp.float32),
        ),
        in_specs=[
            pl.BlockSpec((reps, 2, vecs, width), lambda i: (0, 0, 0, i)),
            pl.BlockSpec((reps, pieces, vecs, pot.shape[3]), lambda i: (0, i, 0, 0)),
            pl.BlockSpec((BLK, BLK), lambda i: (0, 0)),
            pl.BlockSpec((1, width), lambda i: (0, i)),
        ],
        out_specs=(
            pl.BlockSpec((count, width), lambda i: (0, i)),
            pl.BlockSpec(packed, lambda i: (0, 0)),
        ),
        scratch_shapes=[pltpu.VMEM((4 * count, 2 * count), jnp.float32)],
        compiler_params=pltpu.CompilerParams(vmem_limit_bytes=VMEM_LIMIT),
        cost_estimate=pl.CostEstimate(
            flops=16 * count * count * rows, bytes_accessed=8 * count * rows, transcendentals=0
        ),
    )(moved, pot, kinetic, precond)


def solve_kernel(full_rows, sums_ref, vector_sums_ref, moved_ref, image_ref, precond_ref, out_ref, rayleigh_ref, mix_ref):
    count = image_ref.shape[0]
    reps, _, vecs, width = moved_ref.shape

    @pl.when(pl.program_id(0) == 0)
    def _():
        turned = sums_ref[count:2 * count, 0:count] / full_rows
        rayleigh = turned.T
        rayleigh_ref[...] = rayleigh
        third = jnp.concatenate([
            sums_ref[2 * count:, b * PAD:(b + 1) * PAD] for b in range(reps)
        ], axis=0)
        mixed = jnp.concatenate(
            [sums_ref[0:count, count:], sums_ref[count:2 * count, count:], third], axis=1
        )
        cross = dot_exact(mixed, rayleigh)
        last = dot_exact(turned, dot_exact(vector_sums_ref[...], rayleigh))
        gram = (sums_ref[0:count, 0:count] - cross - cross.T + last) / full_rows
        pad = jnp.zeros((count, LANES - count), jnp.float32)
        row, column = iota((count, LANES), 0), iota((count, LANES), 1)
        left = jnp.concatenate([gram, pad], axis=1)
        right = jnp.where(row == column, 1.0, 0.0)
        for j in range(count):
            pivot_left, pivot_right = left[j:j + 1, :], right[j:j + 1, :]
            ratio = left[:, j:j + 1] / pivot_left[:, j:j + 1]
            ratio = jnp.where(row[:, 0:1] > j, ratio, 0.0)
            left = left - ratio * pivot_left
            right = right - ratio * pivot_right
        diagonal = jnp.sum(jnp.where(row == column, left, 0.0), axis=1, keepdims=True)
        inverse = (right * lax.rsqrt(diagonal))[:, 0:count]
        parts = three_parts(inverse) + three_parts(-dot_exact(inverse, turned))
        for k in range(3):
            mix_ref[k * count:(k + 1) * count, 0:count] = parts[k]
            mix_ref[k * count:(k + 1) * count, count:2 * count] = parts[3 + k]

    vectors = jnp.concatenate(
        [moved_ref[b, 0].astype(jnp.float32) for b in range(reps)], axis=0
    ).astype(jnp.bfloat16)
    both = jnp.concatenate([image_ref[...], vectors], axis=0)
    chunk = 512
    for s in range(0, width, chunk):
        parts = jnp.dot(mix_ref[...], both[:, s:s + chunk], preferred_element_type=jnp.float32)
        total = (parts[2 * count:] + parts[count:2 * count]) + parts[0:count]
        out_ref[:, 0, s:s + chunk] = total * precond_ref[0:1, s:s + chunk]


def solved_of(sums, vector_sums, moved, image, precond, full_rows, steps):
    reps, _, vecs, rows = moved.shape
    width = rows // steps
    count = reps * vecs
    return pl.pallas_call(
        functools.partial(solve_kernel, full_rows),
        grid=(steps,),
        out_shape=(
            jax.ShapeDtypeStruct((count, 1, rows), jnp.float32),
            jax.ShapeDtypeStruct((count, count), jnp.float32),
        ),
        in_specs=[
            pl.BlockSpec(sums.shape, lambda i: (0, 0)),
            pl.BlockSpec((count, count), lambda i: (0, 0)),
            pl.BlockSpec((reps, 1, vecs, width), lambda i: (0, 0, 0, i)),
            pl.BlockSpec((count, width), lambda i: (0, i)),
            pl.BlockSpec((1, width), lambda i: (0, i)),
        ],
        out_specs=(
            pl.BlockSpec((count, 1, width), lambda i: (0, 0, i)),
            pl.BlockSpec((count, count), lambda i: (0, 0)),
        ),
        scratch_shapes=[pltpu.VMEM((3 * count, 2 * count), jnp.bfloat16)],
        compiler_params=pltpu.CompilerParams(vmem_limit_bytes=VMEM_LIMIT),
        cost_estimate=pl.CostEstimate(
            flops=12 * count * count * rows, bytes_accessed=8 * count * rows, transcendentals=0
        ),
    )(sums, vector_sums, moved, image, precond)


def sum_over_devices(x):
    def turned(axis, stride, shift):
        size = lax.axis_size(axis)
        pairs = []
        for i in range(size):
            digit = (i // stride) % 4
            pairs.append((i, i + ((digit + shift) % 4 - digit) * stride))
        return lax.ppermute(x, axis, pairs)

    x = x + lax.ppermute(x, "row", [(i, i ^ 1) for i in range(lax.axis_size("row"))])
    for axis, stride in (("rep", 1), ("row", 8), ("row", 2)):
        up, down, across = (turned(axis, stride, shift) for shift in (1, 3, 2))
        x = (x + across) + (up + down)
    return x


def body(
    basis_vecs, potential, surface, grid_perm, kinetic, couplings, coupling_coefficient, precond
):
    vecs, rows = basis_vecs.shape
    pieces = lax.axis_size("row")
    reps = lax.axis_size("rep")
    width = rows // pieces
    blocks = rows // BLK
    edge = HB * BLK
    forward = [(i, i + 1) for i in range(pieces - 1)]
    backward = [(i + 1, i) for i in range(pieces - 1)]
    low = lax.ppermute(basis_vecs[:, rows - edge:], "row", forward)
    high = lax.ppermute(basis_vecs[:, :edge], "row", backward)
    by_piece = basis_vecs.reshape(vecs, pieces, width).transpose(1, 0, 2)
    arrived = lax.all_to_all(by_piece, "row", split_axis=0, concat_axis=0, tiled=True)
    columns = couplings[:, 1] - (lax.axis_index("row") * blocks - HB)
    by_rep = source_of(basis_vecs, low, high, columns, coupling_coefficient, reps)
    out, back = index_streams(grid_perm, reps)
    by_rep, out, back = lax.optimization_barrier((by_rep, out, back))
    moved = lax.all_to_all(by_rep, "rep", split_axis=0, concat_axis=0, tiled=True)
    restored = surface_pass(arrived, out, back, potential, surface, reps)
    pot = lax.all_to_all(restored, ("rep", "row"), split_axis=0, concat_axis=0, tiled=True)
    pot = pot.reshape(reps, pieces, vecs, width // reps)
    scale = precond.reshape(1, -1)
    of_vectors = sum_over_devices(vector_sums(moved, scale, 8))
    image, sums = image_of(moved, pot, kinetic, scale, 8)
    sums = sum_over_devices(sums)
    solved, rayleigh = solved_of(sums, of_vectors, moved, image, scale, float(rows * pieces), 8)
    return (solved.reshape(reps * vecs, 1, 1, -1), rayleigh)


def solution(mesh):
    in_specs = (
        P("rep", "row"),
        P("row"),
        P(),
        P("row"),
        P(),
        P("row", None),
        P("row"),
        P("row", "rep", None),
    )
    out_specs = (P(None, "row", "rep", None), P())
    return jax.shard_map(body, mesh=mesh, in_specs=in_specs, out_specs=out_specs, check_vma=False)
```

```python
import functools

import jax
import jax.numpy as jnp
from jax import lax
from jax.experimental import pallas as pl
from jax.experimental.pallas import tpu as pltpu
from jax.sharding import PartitionSpec as P

HB = 2
COUPLINGS_PER_ROW = 3
BLK = 256
PAD = 32
GROUPS = 4
LANES = 128
SPAN = GROUPS * BLK
VMEM_LIMIT = 60 * 2**20
NT = (((1,), (1,)), ((), ()))
WHOLE = pl.BlockSpec(memory_space=pltpu.VMEM)
SCALARS = pl.BlockSpec(memory_space=pltpu.SMEM)


def dot_nt(a, b):
    return lax.dot_general(a, b, NT, preferred_element_type=jnp.float32)


def dot_exact(a, b):
    return jnp.dot(a, b, precision=lax.Precision.HIGHEST, preferred_element_type=jnp.float32)


def iota(shape, dim):
    return lax.broadcasted_iota(jnp.int32, shape, dim)


def three_parts(x):
    high = x.astype(jnp.bfloat16)
    rest = x - high.astype(jnp.float32)
    middle = rest.astype(jnp.bfloat16)
    low = (rest - middle.astype(jnp.float32)).astype(jnp.bfloat16)
    return [high, middle, low]


def inverse_kernel(reps, perm_ref, power_ref, out_ref, back_ref, acc_ref):
    blocks = perm_ref.shape[0]
    half = blocks // 2
    step = 4
    rows = iota((BLK, BLK), 0)
    lane = iota((1, BLK), 1)
    code = jnp.where(lane < 128, lane + 128, -lane).astype(jnp.float32)

    for part in range(2):
        mine = slice(part * BLK, (part + 1) * BLK)
        acc_ref[mine, :] = jnp.zeros((BLK, BLK), jnp.float32)

        @pl.loop(0, half // 8)
        def _(i):
            tile = perm_ref[pl.ds(pl.multiple_of(part * half + i * 8, 8), 8), :]
            high = tile >> 8
            low = tile & 255
            for first in range(0, 8, step):
                left, right = [], []
                for k in range(first, first + step):
                    value = code * power_ref[i * 8 + k]
                    left.append(
                        jnp.where(rows == high[k:k + 1, :], value, 0.0).astype(jnp.bfloat16)
                    )
                    right.append(
                        jnp.where(rows == low[k:k + 1, :], 1.0, 0.0).astype(jnp.bfloat16)
                    )
                acc_ref[mine, :] += dot_nt(
                    jnp.concatenate(left, axis=1), jnp.concatenate(right, axis=1)
                )

    for r in range(0, BLK, 32):
        late = acc_ref[BLK + r:BLK + r + 32, :]
        held = acc_ref[r:r + 32, :] + late
        size = jnp.abs(held)
        number = jnp.where(late != 0.0, 32768.0, 0.0) + jnp.where(held < 0.0, 128.0, 0.0)
        for bit in (64, 32, 16, 8, 4, 2, 1):
            above = size >= 2.0 ** (bit - 57)
            size = jnp.where(above, size * 2.0 ** -bit, size)
            number = number + jnp.where(above, bit * 256.0, 0.0)
        acc_ref[r:r + 32, :] = number + (size * 2.0 ** 64 - 128.0)

    per_rep = 8 // reps
    for d in range(blocks // 8):
        tile = acc_ref[d * 8:(d + 1) * 8, :]
        for b in range(reps):
            start = BLK + b * (blocks // reps) + d * per_rep
            acc_ref[start:start + per_rep, :] = tile[b * per_rep:(b + 1) * per_rep, :]
    for k in range(2):
        out_ref[k * BLK:(k + 1) * BLK, :] = perm_ref[k * half:(k + 1) * half, :].T
        back_ref[k * BLK:(k + 1) * BLK, :] = acc_ref[
            BLK + k * half:BLK + (k + 1) * half, :
        ].T.astype(jnp.int32)


def index_streams(perm, reps):
    blocks = perm.shape[0] // BLK
    streams = jax.ShapeDtypeStruct((2 * BLK, blocks // 2), jnp.int32)
    powers = jnp.asarray([2.0 ** (k - 64) for k in range(blocks // 2)], jnp.float32)
    out, back = pl.pallas_call(
        functools.partial(inverse_kernel, reps),
        out_shape=(streams, streams),
        in_specs=[WHOLE, SCALARS],
        out_specs=(WHOLE, WHOLE),
        scratch_shapes=[pltpu.VMEM((2 * BLK, BLK), jnp.float32)],
        compiler_params=pltpu.CompilerParams(vmem_limit_bytes=VMEM_LIMIT),
        cost_estimate=pl.CostEstimate(
            flops=2 * BLK * BLK * blocks * BLK, bytes_accessed=8 * blocks * BLK, transcendentals=0
        ),
    )(perm.reshape(blocks, BLK), powers)
    return out.reshape(-1), back.reshape(-1)


def stream(index_ref, streams, sem, table_ref, rows_refs, work):
    sublane = iota((8, LANES), 0)
    size = streams[0].shape[0]
    half = size // 8
    count = half // 2
    copies = [
        pltpu.make_async_copy(index_ref.at[pl.ds(k * size, size)], held, sem.at[k])
        for k, held in enumerate(streams)
    ]

    def gather(i, rows_ref):
        def tile(held, places):
            value = None
            for t in range(8):
                row = jnp.broadcast_to(table_ref[pl.ds(held[places[t]], 1), :], (8, LANES))
                value = row if value is None else jnp.where(sublane == t, row, value)
            return value

        for part in range(2):
            places = [t * half + 2 * i + part for t in range(8)]
            for k in range(0, len(streams), 2):
                both = jnp.concatenate([tile(held, places) for held in streams[k:k + 2]], axis=0)
                first = part * len(streams) * 8 + k * 8
                rows_ref[first:first + 16, :] = both.astype(jnp.bfloat16)

    def begin():
        for copy in copies:
            copy.start()

    def run():
        for copy in copies:
            copy.wait()
        gather(0, rows_refs[0])

        @pl.loop(0, count // 2)
        def _(j):
            for s in range(2):
                i = j * 2 + s
                gather(jnp.minimum(i + 1, count - 1), rows_refs[(s + 1) % 2])
                work(i, rows_refs[s % 2])

    return begin, run


def blocks_of(i, blocks):
    return [2 * i, 2 * i + blocks // 2, 2 * i + 1, 2 * i + 1 + blocks // 2]


def surface_kernel(
    x_ref, perm_ref, back_ref, pot_ref, surf_ref, out_ref,
    table_ref, packed_ref, even_ref, odd_ref, *rest
):
    streams, sem = rest[:-1], rest[-1]
    pieces, vecs, width = x_ref.shape
    points = table_ref.shape[0]
    per_group = pieces // GROUPS
    group_rows = points // GROUPS
    row, column = iota((LANES, GROUPS * LANES), 0), iota((LANES, GROUPS * LANES), 1)
    fold = jnp.where(
        (row // PAD == column // LANES) & (row % PAD == column % PAD), 1.0, 0.0
    ).astype(jnp.bfloat16)
    unit = jnp.where(iota((BLK, BLK), 0) == iota((BLK, BLK), 1), 1.0, 0.0).astype(jnp.bfloat16)
    lane_group = iota((BLK, LANES), 1) // PAD
    count = points // SPAN
    blocks = points // BLK

    def folded(rows_ref):
        wide = jnp.concatenate([rows_ref[q * BLK:(q + 1) * BLK, :] for q in range(GROUPS)], axis=1)
        return dot_nt(fold, wide)

    def spread(rows, starts):
        for q in range(GROUPS):
            table_ref[pl.ds(pl.multiple_of(starts[q], BLK), BLK), :] = jnp.where(
                lane_group == q, rows, 0.0
            )

    def to_grid_and_back(i, rows_ref):
        values = folded(rows_ref).astype(jnp.bfloat16)
        projected = jnp.dot(values, surf_ref[...], preferred_element_type=jnp.float32)
        weighted = jnp.concatenate([
            projected[q * PAD:(q + 1) * PAD] * pot_ref[pl.ds(block, 1), :]
            for q, block in enumerate(blocks_of(i, blocks))
        ], axis=0).astype(jnp.bfloat16)
        returned = dot_nt(surf_ref[...], weighted).astype(jnp.bfloat16).astype(jnp.float32)
        packed_ref[pl.ds(pl.multiple_of(i * BLK, BLK), BLK), :] = returned

    def to_basis(i, rows_ref):
        values = folded(rows_ref).astype(jnp.bfloat16)
        per_piece = out_ref.shape[2] // BLK
        for q in range(GROUPS):
            at = (q // per_piece) * BLK
            out_ref[i + (q % per_piece) * (out_ref.shape[0] // per_piece), :, at:at + BLK] = values[
                q * PAD:q * PAD + vecs
            ]

    begin, run = stream(perm_ref, streams, sem, table_ref, (even_ref, odd_ref), to_grid_and_back)
    begin()
    chunk = 512

    @pl.loop(0, per_group)
    def _(d):
        for c in range(0, width, chunk):
            parts = []
            for q in range(GROUPS):
                parts.append(x_ref[q * per_group + d, :, c:c + chunk].astype(jnp.float32))
                parts.append(jnp.zeros((PAD - vecs, chunk), jnp.float32))
            stacked = jnp.concatenate(parts, axis=0).astype(jnp.bfloat16)
            for h in range(0, chunk, BLK):
                rows = dot_nt(unit, stacked[:, h:h + BLK])
                spread(rows, [q * group_rows + d * width + c + h for q in range(GROUPS)])

    run()
    begin, run = stream(back_ref, streams, sem, table_ref, (even_ref, odd_ref), to_basis)
    begin()

    @pl.loop(0, count)
    def _(i):
        rows = packed_ref[pl.ds(pl.multiple_of(i * BLK, BLK), BLK), :]
        spread(rows, [block * BLK for block in blocks_of(i, blocks)])

    run()


def surface_pass(arrived, perm, back, potential, surface, reps):
    pieces, vecs, width = arrived.shape
    points = perm.shape[0]
    return pl.pallas_call(
        surface_kernel,
        out_shape=jax.ShapeDtypeStruct((pieces * reps, vecs, width // reps), jnp.bfloat16),
        in_specs=[WHOLE] * 5,
        out_specs=WHOLE,
        scratch_shapes=[
            pltpu.VMEM((points, LANES), jnp.float32),
            pltpu.VMEM((points // GROUPS, LANES), jnp.float32),
            pltpu.VMEM((SPAN, LANES), jnp.bfloat16),
            pltpu.VMEM((SPAN, LANES), jnp.bfloat16),
        ] + [pltpu.SMEM((4 * BLK,), jnp.int32)] * 64 + [pltpu.SemaphoreType.DMA((64,))],
        compiler_params=pltpu.CompilerParams(vmem_limit_bytes=VMEM_LIMIT),
        cost_estimate=pl.CostEstimate(
            flops=4 * vecs * points * BLK, bytes_accessed=300_000_000, transcendentals=0
        ),
    )(arrived, perm, back, potential.reshape(-1, BLK), surface)


def source_kernel(vecs_ref, low_ref, high_ref, column_ref, weight_ref, out_ref, wide_ref):
    reps = out_ref.shape[0]
    edge = low_ref.shape[1]
    rows = vecs_ref.shape[1]
    blocks = rows // BLK
    piece_blocks = out_ref.shape[3] * reps // (blocks * BLK)
    wide_ref[:, 0:edge] = low_ref[...]
    wide_ref[:, edge + rows:] = high_ref[...]
    per_piece = 8
    per_rep = per_piece // reps

    @pl.loop(0, blocks // per_piece)
    def _(j):
        start = pl.multiple_of(j * per_piece * BLK, per_piece * BLK)
        wide_ref[:, pl.ds(edge + start, per_piece * BLK)] = vecs_ref[:, pl.ds(start, per_piece * BLK)]

    @pl.loop(0, blocks // per_piece)
    def _(j):
        for k in range(per_piece):
            a = j * per_piece + k
            total = None
            for m in range(COUPLINGS_PER_ROW):
                c = a * COUPLINGS_PER_ROW + m
                at = pl.multiple_of(column_ref[c] * BLK, BLK)
                term = wide_ref[:, pl.ds(at, BLK)].astype(jnp.float32) * weight_ref[c]
                total = term if total is None else total + term
            to = pl.ds(pl.multiple_of(j * per_rep * BLK, per_rep * BLK) + (k % per_rep) * BLK, BLK)
            here = pl.multiple_of(a * BLK, BLK)
            out_ref[k // per_rep, 0, :, to] = vecs_ref[:, pl.ds(here, BLK)]
            out_ref[k // per_rep, 1, :, to] = total.astype(jnp.bfloat16)


def source_of(basis_vecs, low, high, columns, weights, reps):
    vecs, rows = basis_vecs.shape
    return pl.pallas_call(
        source_kernel,
        out_shape=jax.ShapeDtypeStruct((reps, 2, vecs, rows // reps), jnp.bfloat16),
        in_specs=[WHOLE, WHOLE, WHOLE, SCALARS, SCALARS],
        out_specs=WHOLE,
        scratch_shapes=[pltpu.VMEM((vecs, rows + 2 * low.shape[1]), jnp.bfloat16)],
        compiler_params=pltpu.CompilerParams(vmem_limit_bytes=VMEM_LIMIT),
        cost_estimate=pl.CostEstimate(
            flops=6 * vecs * rows, bytes_accessed=12 * vecs * rows, transcendentals=0
        ),
    )(basis_vecs, low, high, columns, weights)


def image_kernel(
    core_ref, moved_ref, pot_ref, kinetic_ref, precond_ref,
    image_ref, keep_ref, give_ref, total_ref, vector_ref, sums_ref
):
    step = pl.program_id(0)
    reps, _, vecs, width = moved_ref.shape
    segment = pot_ref.shape[3]
    count = reps * vecs

    @pl.when(step == 0)
    def _():
        total_ref[...] = jnp.zeros_like(total_ref)
        vector_ref[...] = jnp.zeros_like(vector_ref)

    def joined(k, at):
        parts = [moved_ref[b, k, :, at].astype(jnp.float32) for b in range(reps)]
        return jnp.concatenate(parts, axis=0).astype(jnp.bfloat16)

    source = joined(1, slice(0, width))
    blocks = [source[:, h:h + BLK] for h in range(0, width, BLK)]
    kin_blocks = jnp.dot(
        jnp.concatenate(blocks, axis=0), kinetic_ref[...], preferred_element_type=jnp.float32
    )
    per_segment = segment // BLK

    for s in range(width // segment):
        at = slice(s * segment, (s + 1) * segment)
        vectors = joined(0, at)
        kin = jnp.concatenate([
            kin_blocks[h * count:(h + 1) * count]
            for h in range(s * per_segment, (s + 1) * per_segment)
        ], axis=1)
        pot = jnp.concatenate([pot_ref[b, s].astype(jnp.float32) for b in range(reps)], axis=0)
        image = (kin + pot).astype(jnp.bfloat16)
        image_ref[:, at] = image
        scale = precond_ref[0:1, at]
        square = scale * scale
        scaled = three_parts(image.astype(jnp.float32) * square)
        left = jnp.concatenate(scaled + [image], axis=0)
        total_ref[...] += dot_nt(left, jnp.concatenate([image, vectors], axis=0))
        scaled = three_parts(vectors.astype(jnp.float32) * square)
        vector_ref[...] += dot_nt(jnp.concatenate(scaled, axis=0), vectors)

    @pl.when(step == pl.num_programs(0) - 1)
    def _():
        scaled = total_ref[0:count] + total_ref[count:2 * count] + total_ref[2 * count:3 * count]
        own, cross = scaled[:, 0:count], scaled[:, count:2 * count]
        plain = total_ref[3 * count:4 * count, count:2 * count]
        vector = vector_ref[0:count] + vector_ref[count:2 * count] + vector_ref[2 * count:3 * count]
        row, column = iota((count, count), 0), iota((count, count), 1)
        own = jnp.where(row <= column, own, vector)
        diagonal = jnp.sum(jnp.where(row == column, vector, 0.0), axis=0, keepdims=True)
        sums_ref[0:count, :] = jnp.concatenate([own, cross[:, 0:PAD]], axis=1)
        sums_ref[count:2 * count, :] = jnp.concatenate([plain, cross[:, PAD:2 * PAD]], axis=1)
        sums_ref[2 * count:2 * count + vecs, :] = jnp.concatenate(
            [cross[b * vecs:(b + 1) * vecs, 2 * PAD:3 * PAD] for b in range(reps)], axis=1
        )
        sums_ref[2 * count + vecs:, :] = jnp.broadcast_to(
            jnp.concatenate([diagonal, jnp.zeros((1, PAD), jnp.float32)], axis=1), (8, LANES)
        )
        size = keep_ref.shape[0]
        core = core_ref[0]
        keep_ref[...] = sums_ref[pl.ds(pl.multiple_of(core * size, 8), size), :]
        give_ref[...] = sums_ref[pl.ds(pl.multiple_of((1 - core) * size, 8), size), :]


def image_of(core, moved, pot, kinetic, precond, steps):
    reps, _, vecs, rows = moved.shape
    width = rows // steps
    count = reps * vecs
    pieces = pot.shape[1] // steps
    packed = (2 * count + vecs + 8, LANES)
    half = (packed[0] // 2, LANES)
    return pl.pallas_call(
        image_kernel,
        grid=(steps,),
        out_shape=(
            jax.ShapeDtypeStruct((count, rows), jnp.bfloat16),
            jax.ShapeDtypeStruct(half, jnp.float32),
            jax.ShapeDtypeStruct(half, jnp.float32),
        ),
        in_specs=[
            SCALARS,
            pl.BlockSpec((reps, 2, vecs, width), lambda i: (0, 0, 0, i)),
            pl.BlockSpec((reps, pieces, vecs, pot.shape[3]), lambda i: (0, i, 0, 0)),
            pl.BlockSpec((BLK, BLK), lambda i: (0, 0)),
            pl.BlockSpec((1, width), lambda i: (0, i)),
        ],
        out_specs=(
            pl.BlockSpec((count, width), lambda i: (0, i)),
            pl.BlockSpec(half, lambda i: (0, 0)),
            pl.BlockSpec(half, lambda i: (0, 0)),
        ),
        scratch_shapes=[
            pltpu.VMEM((4 * count, 2 * count), jnp.float32),
            pltpu.VMEM((3 * count, count), jnp.float32),
            pltpu.VMEM(packed, jnp.float32),
        ],
        compiler_params=pltpu.CompilerParams(vmem_limit_bytes=VMEM_LIMIT),
        cost_estimate=pl.CostEstimate(
            flops=22 * count * count * rows, bytes_accessed=8 * count * rows, transcendentals=0
        ),
    )(core, moved, pot, kinetic, precond)


def solve_kernel(
    full_rows, core_ref, mine_ref, other_ref, moved_ref, image_ref, precond_ref,
    out_ref, rayleigh_ref, mix_ref, sums_ref
):
    count = image_ref.shape[0]
    reps, _, vecs, width = moved_ref.shape

    @pl.when(pl.program_id(0) == 0)
    def _():
        size = mine_ref.shape[0]
        core = core_ref[0]
        sums_ref[pl.ds(pl.multiple_of(core * size, 8), size), :] = mine_ref[...]
        sums_ref[pl.ds(pl.multiple_of((1 - core) * size, 8), size), :] = other_ref[...]
        row, column = iota((count, count), 0), iota((count, count), 1)
        shared = sums_ref[0:count, 0:count]
        shared_t = shared.T
        own = jnp.where(row <= column, shared, shared_t)
        vector = jnp.where(row <= column, shared_t, shared)
        diagonal = sums_ref[2 * count + vecs:2 * count + vecs + 1, 0:count]
        vector = jnp.where(row == column, diagonal, vector)
        turned = sums_ref[count:2 * count, 0:count] / full_rows
        rayleigh = turned.T
        rayleigh_ref[...] = rayleigh
        third = jnp.concatenate([
            sums_ref[2 * count:2 * count + vecs, b * PAD:(b + 1) * PAD] for b in range(reps)
        ], axis=0)
        mixed = jnp.concatenate(
            [sums_ref[0:count, count:], sums_ref[count:2 * count, count:], third], axis=1
        )
        cross = dot_exact(mixed, rayleigh)
        last = dot_exact(turned, dot_exact(vector, rayleigh))
        gram = (own - cross - cross.T + last) / full_rows
        pad = jnp.zeros((count, LANES - count), jnp.float32)
        row, column = iota((count, LANES), 0), iota((count, LANES), 1)
        left = jnp.concatenate([gram, pad], axis=1)
        right = jnp.where(row == column, 1.0, 0.0)
        for j in range(0, count, 2):
            first, second = left[j:j + 1, :], left[j + 1:j + 2, :]
            a, b, c = first[:, j:j + 1], first[:, j + 1:j + 2], second[:, j + 1:j + 2]
            over = 1.0 / (a * c - b * b)
            below = row[:, 0:1] > j + 1
            one, two = left[:, j:j + 1], left[:, j + 1:j + 2]
            ratio_one = jnp.where(below, (one * c - two * b) * over, 0.0)
            ratio_two = jnp.where(below, (two * a - one * b) * over, 0.0)
            left = left - (ratio_one * first + ratio_two * second)
            right = right - (ratio_one * right[j:j + 1, :] + ratio_two * right[j + 1:j + 2, :])
        diagonal = jnp.sum(jnp.where(row == column, left, 0.0), axis=1, keepdims=True)
        beside = jnp.sum(jnp.where(row == column + 1, left, 0.0), axis=1, keepdims=True)
        diagonal = jnp.broadcast_to(diagonal, left.shape)
        ratio = jnp.where(row % 2 == 1, beside / pltpu.roll(diagonal, 1, 0), 0.0)
        right = right - ratio * pltpu.roll(right, 1, 0)
        inverse = (right * lax.rsqrt(diagonal - ratio * beside))[:, 0:count]
        parts = three_parts(inverse) + three_parts(-dot_exact(inverse, turned))
        for k in range(3):
            mix_ref[k * count:(k + 1) * count, 0:count] = parts[k]
            mix_ref[k * count:(k + 1) * count, count:2 * count] = parts[3 + k]

    vectors = jnp.concatenate(
        [moved_ref[b, 0].astype(jnp.float32) for b in range(reps)], axis=0
    ).astype(jnp.bfloat16)
    both = jnp.concatenate([image_ref[...], vectors], axis=0)
    chunk = 512
    for s in range(0, width, chunk):
        parts = jnp.dot(mix_ref[...], both[:, s:s + chunk], preferred_element_type=jnp.float32)
        total = (parts[2 * count:] + parts[count:2 * count]) + parts[0:count]
        out_ref[:, 0, s:s + chunk] = total * precond_ref[0:1, s:s + chunk]


def solved_of(core, mine, other, moved, image, precond, full_rows, steps):
    reps, _, vecs, rows = moved.shape
    width = rows // steps
    count = reps * vecs
    return pl.pallas_call(
        functools.partial(solve_kernel, full_rows),
        grid=(steps,),
        out_shape=(
            jax.ShapeDtypeStruct((count, 1, rows), jnp.float32),
            jax.ShapeDtypeStruct((count, count), jnp.float32),
        ),
        in_specs=[
            SCALARS,
            pl.BlockSpec(mine.shape, lambda i: (0, 0)),
            pl.BlockSpec(mine.shape, lambda i: (0, 0)),
            pl.BlockSpec((reps, 1, vecs, width), lambda i: (0, 0, 0, i)),
            pl.BlockSpec((count, width), lambda i: (0, i)),
            pl.BlockSpec((1, width), lambda i: (0, i)),
        ],
        out_specs=(
            pl.BlockSpec((count, 1, width), lambda i: (0, 0, i)),
            pl.BlockSpec((count, count), lambda i: (0, 0)),
        ),
        scratch_shapes=[
            pltpu.VMEM((3 * count, 2 * count), jnp.bfloat16),
            pltpu.VMEM((2 * mine.shape[0], LANES), jnp.float32),
        ],
        compiler_params=pltpu.CompilerParams(vmem_limit_bytes=VMEM_LIMIT),
        cost_estimate=pl.CostEstimate(
            flops=12 * count * count * rows, bytes_accessed=8 * count * rows, transcendentals=0
        ),
    )(core, mine, other, moved, image, precond)


def sum_over_devices(keep, give):
    def turned(x, axis, stride, shift):
        pairs = []
        for i in range(lax.axis_size(axis)):
            digit = (i // stride) % 4
            pairs.append((i, i + ((digit + shift) % 4 - digit) * stride))
        return lax.ppermute(x, axis, pairs)

    swap = [(i, i ^ 1) for i in range(lax.axis_size("row"))]
    x = keep + lax.ppermute(give, "row", swap)
    for axis, stride in (("rep", 1), ("row", 8), ("row", 2)):
        up, down, across = (turned(x, axis, stride, shift) for shift in (1, 3, 2))
        x = (x + across) + (up + down)
    return x, lax.ppermute(x, "row", swap)


def body(
    basis_vecs, potential, surface, grid_perm, kinetic, couplings, coupling_coefficient, precond
):
    vecs, rows = basis_vecs.shape
    pieces = lax.axis_size("row")
    reps = lax.axis_size("rep")
    width = rows // pieces
    blocks = rows // BLK
    edge = HB * BLK
    forward = [(i, i + 1) for i in range(pieces - 1)]
    backward = [(i + 1, i) for i in range(pieces - 1)]
    low = lax.ppermute(basis_vecs[:, rows - edge:], "row", forward)
    high = lax.ppermute(basis_vecs[:, :edge], "row", backward)
    by_piece = basis_vecs.reshape(vecs, pieces, width).transpose(1, 0, 2)
    arrived = lax.all_to_all(by_piece, "row", split_axis=0, concat_axis=0, tiled=True)
    columns = couplings[:, 1] - (lax.axis_index("row") * blocks - HB)
    by_rep = source_of(basis_vecs, low, high, columns, coupling_coefficient, reps)
    out, back = index_streams(grid_perm, reps)
    by_rep, out, back = lax.optimization_barrier((by_rep, out, back))
    moved = lax.all_to_all(by_rep, "rep", split_axis=0, concat_axis=0, tiled=True)
    restored = surface_pass(arrived, out, back, potential, surface, reps)
    pot = lax.all_to_all(restored, ("rep", "row"), split_axis=0, concat_axis=0, tiled=True)
    pot = pot.reshape(reps, pieces, vecs, width // reps)
    scale = precond.reshape(1, -1)
    core = (lax.axis_index("row") % 2).reshape(1)
    image, keep, give = image_of(core, moved, pot, kinetic, scale, 8)
    mine, other = sum_over_devices(keep, give)
    solved, rayleigh = solved_of(core, mine, other, moved, image, scale, float(rows * pieces), 8)
    return (solved.reshape(reps * vecs, 1, 1, -1), rayleigh)


def solution(mesh):
    in_specs = (
        P("rep", "row"),
        P("row"),
        P(),
        P("row"),
        P(),
        P("row", None),
        P("row"),
        P("row", "rep", None),
    )
    out_specs = (P(None, "row", "rep", None), P())
    return jax.shard_map(body, mesh=mesh, in_specs=in_specs, out_specs=out_specs, check_vma=False)
```

```python
import functools

import jax
import jax.numpy as jnp
from jax import lax
from jax.experimental import pallas as pl
from jax.experimental.pallas import tpu as pltpu
from jax.sharding import PartitionSpec as P

HB = 2
COUPLINGS_PER_ROW = 3
BLK = 256
PAD = 32
GROUPS = 4
LANES = 128
SPAN = GROUPS * BLK
VMEM_LIMIT = 60 * 2**20
NT = (((1,), (1,)), ((), ()))
WHOLE = pl.BlockSpec(memory_space=pltpu.VMEM)
SCALARS = pl.BlockSpec(memory_space=pltpu.SMEM)


def dot_nt(a, b):
    return lax.dot_general(a, b, NT, preferred_element_type=jnp.float32)


def dot_exact(a, b):
    return jnp.dot(a, b, precision=lax.Precision.HIGHEST, preferred_element_type=jnp.float32)


def iota(shape, dim):
    return lax.broadcasted_iota(jnp.int32, shape, dim)


def three_parts(x):
    high = x.astype(jnp.bfloat16)
    rest = x - high.astype(jnp.float32)
    middle = rest.astype(jnp.bfloat16)
    low = (rest - middle.astype(jnp.float32)).astype(jnp.bfloat16)
    return [high, middle, low]


def inverse_kernel(reps, perm_ref, power_ref, out_ref, back_ref, acc_ref):
    blocks = perm_ref.shape[0]
    half = blocks // 2
    step = 4
    rows = iota((BLK, BLK), 0)
    lane = iota((1, BLK), 1)
    code = jnp.where(lane < 128, lane + 128, -lane).astype(jnp.float32)

    for part in range(2):
        mine = slice(part * BLK, (part + 1) * BLK)
        acc_ref[mine, :] = jnp.zeros((BLK, BLK), jnp.float32)

        @pl.loop(0, half // 8)
        def _(i):
            tile = perm_ref[pl.ds(pl.multiple_of(part * half + i * 8, 8), 8), :]
            high = tile >> 8
            low = tile & 255
            for first in range(0, 8, step):
                left, right = [], []
                for k in range(first, first + step):
                    value = code * power_ref[i * 8 + k]
                    left.append(
                        jnp.where(rows == high[k:k + 1, :], value, 0.0).astype(jnp.bfloat16)
                    )
                    right.append(
                        jnp.where(rows == low[k:k + 1, :], 1.0, 0.0).astype(jnp.bfloat16)
                    )
                acc_ref[mine, :] += dot_nt(
                    jnp.concatenate(left, axis=1), jnp.concatenate(right, axis=1)
                )

    for r in range(0, BLK, 32):
        late = acc_ref[BLK + r:BLK + r + 32, :]
        held = acc_ref[r:r + 32, :] + late
        size = jnp.abs(held)
        number = jnp.where(late != 0.0, 32768.0, 0.0) + jnp.where(held < 0.0, 128.0, 0.0)
        for bit in (64, 32, 16, 8, 4, 2, 1):
            above = size >= 2.0 ** (bit - 57)
            size = jnp.where(above, size * 2.0 ** -bit, size)
            number = number + jnp.where(above, bit * 256.0, 0.0)
        acc_ref[r:r + 32, :] = number + (size * 2.0 ** 64 - 128.0)

    per_rep = 8 // reps
    for d in range(blocks // 8):
        tile = acc_ref[d * 8:(d + 1) * 8, :]
        for b in range(reps):
            start = BLK + b * (blocks // reps) + d * per_rep
            acc_ref[start:start + per_rep, :] = tile[b * per_rep:(b + 1) * per_rep, :]
    for k in range(2):
        out_ref[k * BLK:(k + 1) * BLK, :] = perm_ref[k * half:(k + 1) * half, :].T
        back_ref[k * BLK:(k + 1) * BLK, :] = acc_ref[
            BLK + k * half:BLK + (k + 1) * half, :
        ].T.astype(jnp.int32)


def index_streams(perm, reps):
    blocks = perm.shape[0] // BLK
    streams = jax.ShapeDtypeStruct((2 * BLK, blocks // 2), jnp.int32)
    powers = jnp.asarray([2.0 ** (k - 64) for k in range(blocks // 2)], jnp.float32)
    out, back = pl.pallas_call(
        functools.partial(inverse_kernel, reps),
        out_shape=(streams, streams),
        in_specs=[WHOLE, SCALARS],
        out_specs=(WHOLE, WHOLE),
        scratch_shapes=[pltpu.VMEM((2 * BLK, BLK), jnp.float32)],
        compiler_params=pltpu.CompilerParams(vmem_limit_bytes=VMEM_LIMIT),
        cost_estimate=pl.CostEstimate(
            flops=2 * BLK * BLK * blocks * BLK, bytes_accessed=8 * blocks * BLK, transcendentals=0
        ),
    )(perm.reshape(blocks, BLK), powers)
    return out.reshape(-1), back.reshape(-1)


def stream(index_ref, streams, sem, table_ref, rows_refs, work):
    sublane = iota((8, LANES), 0)
    size = streams[0].shape[0]
    half = size // 8
    count = half // 2
    copies = [
        pltpu.make_async_copy(index_ref.at[pl.ds(k * size, size)], held, sem.at[k])
        for k, held in enumerate(streams)
    ]

    def gather(i, rows_ref):
        def tile(held, places):
            value = None
            for t in range(8):
                row = jnp.broadcast_to(table_ref[pl.ds(held[places[t]], 1), :], (8, LANES))
                value = row if value is None else jnp.where(sublane == t, row, value)
            return value

        for part in range(2):
            places = [t * half + 2 * i + part for t in range(8)]
            for k in range(0, len(streams), 2):
                both = jnp.concatenate([tile(held, places) for held in streams[k:k + 2]], axis=0)
                first = part * len(streams) * 8 + k * 8
                rows_ref[first:first + 16, :] = both.astype(jnp.bfloat16)

    def begin():
        for copy in copies:
            copy.start()

    def run():
        for copy in copies:
            copy.wait()
        gather(0, rows_refs[0])

        @pl.loop(0, count // 2)
        def _(j):
            for s in range(2):
                i = j * 2 + s
                gather(jnp.minimum(i + 1, count - 1), rows_refs[(s + 1) % 2])
                work(i, rows_refs[s % 2])

    return begin, run


def blocks_of(i, blocks):
    return [2 * i, 2 * i + blocks // 2, 2 * i + 1, 2 * i + 1 + blocks // 2]


def surface_kernel(
    x_ref, perm_ref, back_ref, pot_ref, surf_ref, out_ref,
    table_ref, packed_ref, even_ref, odd_ref, *rest
):
    streams, sem = rest[:-1], rest[-1]
    pieces, vecs, width = x_ref.shape
    points = table_ref.shape[0]
    per_group = pieces // GROUPS
    group_rows = points // GROUPS
    row, column = iota((LANES, GROUPS * LANES), 0), iota((LANES, GROUPS * LANES), 1)
    fold = jnp.where(
        (row // PAD == column // LANES) & (row % PAD == column % PAD), 1.0, 0.0
    ).astype(jnp.bfloat16)
    unit = jnp.where(iota((BLK, BLK), 0) == iota((BLK, BLK), 1), 1.0, 0.0).astype(jnp.bfloat16)
    lane_group = iota((BLK, LANES), 1) // PAD
    count = points // SPAN
    blocks = points // BLK

    def folded(rows_ref):
        wide = jnp.concatenate([rows_ref[q * BLK:(q + 1) * BLK, :] for q in range(GROUPS)], axis=1)
        return dot_nt(fold, wide)

    def spread(rows, starts):
        for q in range(GROUPS):
            table_ref[pl.ds(pl.multiple_of(starts[q], BLK), BLK), :] = jnp.where(
                lane_group == q, rows, 0.0
            )

    def to_grid_and_back(i, rows_ref):
        values = folded(rows_ref).astype(jnp.bfloat16)
        projected = jnp.dot(values, surf_ref[...], preferred_element_type=jnp.float32)
        weighted = jnp.concatenate([
            projected[q * PAD:(q + 1) * PAD] * pot_ref[pl.ds(block, 1), :]
            for q, block in enumerate(blocks_of(i, blocks))
        ], axis=0).astype(jnp.bfloat16)
        returned = dot_nt(surf_ref[...], weighted).astype(jnp.bfloat16).astype(jnp.float32)
        packed_ref[pl.ds(pl.multiple_of(i * BLK, BLK), BLK), :] = returned

    def to_basis(i, rows_ref):
        values = folded(rows_ref).astype(jnp.bfloat16)
        per_piece = out_ref.shape[2] // BLK
        for q in range(GROUPS):
            at = (q // per_piece) * BLK
            out_ref[i + (q % per_piece) * (out_ref.shape[0] // per_piece), :, at:at + BLK] = values[
                q * PAD:q * PAD + vecs
            ]

    begin, run = stream(perm_ref, streams, sem, table_ref, (even_ref, odd_ref), to_grid_and_back)
    begin()
    chunk = 512

    @pl.loop(0, per_group)
    def _(d):
        for c in range(0, width, chunk):
            parts = []
            for q in range(GROUPS):
                parts.append(x_ref[q * per_group + d, :, c:c + chunk].astype(jnp.float32))
                parts.append(jnp.zeros((PAD - vecs, chunk), jnp.float32))
            stacked = jnp.concatenate(parts, axis=0).astype(jnp.bfloat16)
            for h in range(0, chunk, BLK):
                rows = dot_nt(unit, stacked[:, h:h + BLK])
                spread(rows, [q * group_rows + d * width + c + h for q in range(GROUPS)])

    run()
    begin, run = stream(back_ref, streams, sem, table_ref, (even_ref, odd_ref), to_basis)
    begin()

    @pl.loop(0, count)
    def _(i):
        rows = packed_ref[pl.ds(pl.multiple_of(i * BLK, BLK), BLK), :]
        spread(rows, [block * BLK for block in blocks_of(i, blocks)])

    run()


def surface_pass(arrived, perm, back, potential, surface, reps):
    pieces, vecs, width = arrived.shape
    points = perm.shape[0]
    return pl.pallas_call(
        surface_kernel,
        out_shape=jax.ShapeDtypeStruct((pieces * reps, vecs, width // reps), jnp.bfloat16),
        in_specs=[WHOLE] * 5,
        out_specs=WHOLE,
        scratch_shapes=[
            pltpu.VMEM((points, LANES), jnp.float32),
            pltpu.VMEM((points // GROUPS, LANES), jnp.float32),
            pltpu.VMEM((SPAN, LANES), jnp.bfloat16),
            pltpu.VMEM((SPAN, LANES), jnp.bfloat16),
        ] + [pltpu.SMEM((4 * BLK,), jnp.int32)] * 64 + [pltpu.SemaphoreType.DMA((64,))],
        compiler_params=pltpu.CompilerParams(vmem_limit_bytes=VMEM_LIMIT),
        cost_estimate=pl.CostEstimate(
            flops=4 * vecs * points * BLK, bytes_accessed=300_000_000, transcendentals=0
        ),
    )(arrived, perm, back, potential.reshape(-1, BLK), surface)


def source_kernel(rep_ref, vecs_ref, low_ref, high_ref, column_ref, weight_ref, *rest):
    outs, wide_ref = rest[:-1], rest[-1]
    reps = len(outs)
    edge = low_ref.shape[1]
    rows = vecs_ref.shape[1]
    blocks = rows // BLK
    wide_ref[:, 0:edge] = low_ref[...]
    wide_ref[:, edge + rows:] = high_ref[...]
    per_piece = 8
    per_rep = per_piece // reps

    @pl.loop(0, blocks // per_piece)
    def _(j):
        start = pl.multiple_of(j * per_piece * BLK, per_piece * BLK)
        wide_ref[:, pl.ds(edge + start, per_piece * BLK)] = vecs_ref[:, pl.ds(start, per_piece * BLK)]

    @pl.loop(0, blocks // per_piece)
    def _(j):
        for s in range(reps):
            to_rep = (rep_ref[0] + (reps - s)) % reps
            for h in range(per_rep):
                a = j * per_piece + to_rep * per_rep + h
                total = None
                for m in range(COUPLINGS_PER_ROW):
                    c = a * COUPLINGS_PER_ROW + m
                    at = pl.multiple_of(column_ref[c] * BLK, BLK)
                    term = wide_ref[:, pl.ds(at, BLK)].astype(jnp.float32) * weight_ref[c]
                    total = term if total is None else total + term
                to = pl.ds(pl.multiple_of((j * per_rep + h) * BLK, BLK), BLK)
                outs[s][0, :, to] = vecs_ref[:, pl.ds(pl.multiple_of(a * BLK, BLK), BLK)]
                outs[s][1, :, to] = total.astype(jnp.bfloat16)


def source_of(rep, basis_vecs, low, high, columns, weights, reps):
    vecs, rows = basis_vecs.shape
    return pl.pallas_call(
        source_kernel,
        out_shape=(jax.ShapeDtypeStruct((2, vecs, rows // reps), jnp.bfloat16),) * reps,
        in_specs=[SCALARS, WHOLE, WHOLE, WHOLE, SCALARS, SCALARS],
        out_specs=(WHOLE,) * reps,
        scratch_shapes=[pltpu.VMEM((vecs, rows + 2 * low.shape[1]), jnp.bfloat16)],
        compiler_params=pltpu.CompilerParams(vmem_limit_bytes=VMEM_LIMIT),
        cost_estimate=pl.CostEstimate(
            flops=6 * vecs * rows, bytes_accessed=12 * vecs * rows, transcendentals=0
        ),
    )(rep, basis_vecs, low, high, columns, weights)


def vector_kernel(rep_ref, *refs):
    parts = refs[:-6]
    kinetic_ref, precond_ref, vectors_ref, kin_ref, sums_ref, total_ref = refs[-6:]
    step = pl.program_id(0)
    reps = len(parts)
    _, vecs, width = parts[0].shape
    count = reps * vecs

    @pl.when(step == 0)
    def _():
        total_ref[...] = jnp.zeros_like(total_ref)

    def ordered(k):
        for s, part in enumerate(parts):
            group = (rep_ref[0] + s) % reps
            start = pl.multiple_of(group * vecs, 8)
            kin_ref[pl.ds(start, vecs), :] = part[k].astype(jnp.float32)
        return kin_ref[...]

    vectors = ordered(0)
    vectors_16 = vectors.astype(jnp.bfloat16)
    vectors_ref[...] = vectors_16
    scale = precond_ref[...]
    left = jnp.concatenate(three_parts(vectors * (scale * scale)), axis=0)
    total_ref[...] += dot_nt(left, vectors_16)
    source = ordered(1).astype(jnp.bfloat16)
    blocks = [source[:, h:h + BLK] for h in range(0, width, BLK)]
    kin = jnp.dot(jnp.concatenate(blocks, axis=0), kinetic_ref[...], preferred_element_type=jnp.float32)
    for h in range(width // BLK):
        kin_ref[:, h * BLK:(h + 1) * BLK] = kin[h * count:(h + 1) * count]

    @pl.when(step == pl.num_programs(0) - 1)
    def _():
        sums_ref[...] = (
            total_ref[0:count] + total_ref[count:2 * count] + total_ref[2 * count:3 * count]
        )


def vectors_of(rep, parts, kinetic, precond, steps):
    reps = len(parts)
    _, vecs, rows = parts[0].shape
    width = rows // steps
    count = reps * vecs
    return pl.pallas_call(
        vector_kernel,
        grid=(steps,),
        out_shape=(
            jax.ShapeDtypeStruct((count, rows), jnp.bfloat16),
            jax.ShapeDtypeStruct((count, rows), jnp.float32),
            jax.ShapeDtypeStruct((count, count), jnp.float32),
        ),
        in_specs=[SCALARS] + [pl.BlockSpec((2, vecs, width), lambda i: (0, 0, i))] * reps + [
            pl.BlockSpec((BLK, BLK), lambda i: (0, 0)),
            pl.BlockSpec((1, width), lambda i: (0, i)),
        ],
        out_specs=(
            pl.BlockSpec((count, width), lambda i: (0, i)),
            pl.BlockSpec((count, width), lambda i: (0, i)),
            pl.BlockSpec((count, count), lambda i: (0, 0)),
        ),
        scratch_shapes=[pltpu.VMEM((3 * count, count), jnp.float32)],
        compiler_params=pltpu.CompilerParams(vmem_limit_bytes=VMEM_LIMIT),
        cost_estimate=pl.CostEstimate(
            flops=12 * count * count * rows, bytes_accessed=8 * count * rows, transcendentals=0
        ),
    )(rep, *parts, kinetic, precond)


def image_kernel(
    core_ref, vectors_ref, kin_ref, vector_sums_ref, pot_ref, precond_ref,
    image_ref, keep_ref, give_ref, total_ref, sums_ref
):
    step = pl.program_id(0)
    count, width = vectors_ref.shape
    reps, _, vecs, segment = pot_ref.shape

    @pl.when(step == 0)
    def _():
        total_ref[...] = jnp.zeros_like(total_ref)

    for s in range(width // segment):
        at = slice(s * segment, (s + 1) * segment)
        pot = jnp.concatenate([pot_ref[b, s].astype(jnp.float32) for b in range(reps)], axis=0)
        image = (kin_ref[:, at] + pot).astype(jnp.bfloat16)
        image_ref[:, at] = image
        scale = precond_ref[0:1, at]
        scaled = three_parts(image.astype(jnp.float32) * (scale * scale))
        left = jnp.concatenate(scaled + [image], axis=0)
        total_ref[...] += dot_nt(left, jnp.concatenate([image, vectors_ref[:, at]], axis=0))

    @pl.when(step == pl.num_programs(0) - 1)
    def _():
        scaled = total_ref[0:count] + total_ref[count:2 * count] + total_ref[2 * count:3 * count]
        own, cross = scaled[:, 0:count], scaled[:, count:2 * count]
        plain = total_ref[3 * count:4 * count, count:2 * count]
        vector = vector_sums_ref[...]
        row, column = iota((count, count), 0), iota((count, count), 1)
        own = jnp.where(row <= column, own, vector)
        diagonal = jnp.sum(jnp.where(row == column, vector, 0.0), axis=0, keepdims=True)
        sums_ref[0:count, :] = jnp.concatenate([own, cross[:, 0:PAD]], axis=1)
        sums_ref[count:2 * count, :] = jnp.concatenate([plain, cross[:, PAD:2 * PAD]], axis=1)
        sums_ref[2 * count:2 * count + vecs, :] = jnp.concatenate(
            [cross[b * vecs:(b + 1) * vecs, 2 * PAD:3 * PAD] for b in range(reps)], axis=1
        )
        sums_ref[2 * count + vecs:, :] = jnp.broadcast_to(
            jnp.concatenate([diagonal, jnp.zeros((1, PAD), jnp.float32)], axis=1), (8, LANES)
        )
        size = keep_ref.shape[0]
        core = core_ref[0]
        keep_ref[...] = sums_ref[pl.ds(pl.multiple_of(core * size, 8), size), :]
        give_ref[...] = sums_ref[pl.ds(pl.multiple_of((1 - core) * size, 8), size), :]


def image_of(core, vectors, kin, vector_sums, pot, precond, steps):
    count, rows = vectors.shape
    reps, pieces, vecs, segment = pot.shape
    width = rows // steps
    packed = (2 * count + vecs + 8, LANES)
    half = (packed[0] // 2, LANES)
    return pl.pallas_call(
        image_kernel,
        grid=(steps,),
        out_shape=(
            jax.ShapeDtypeStruct((count, rows), jnp.bfloat16),
            jax.ShapeDtypeStruct(half, jnp.float32),
            jax.ShapeDtypeStruct(half, jnp.float32),
        ),
        in_specs=[
            SCALARS,
            pl.BlockSpec((count, width), lambda i: (0, i)),
            pl.BlockSpec((count, width), lambda i: (0, i)),
            pl.BlockSpec((count, count), lambda i: (0, 0)),
            pl.BlockSpec((reps, pieces // steps, vecs, segment), lambda i: (0, i, 0, 0)),
            pl.BlockSpec((1, width), lambda i: (0, i)),
        ],
        out_specs=(
            pl.BlockSpec((count, width), lambda i: (0, i)),
            pl.BlockSpec(half, lambda i: (0, 0)),
            pl.BlockSpec(half, lambda i: (0, 0)),
        ),
        scratch_shapes=[
            pltpu.VMEM((4 * count, 2 * count), jnp.float32),
            pltpu.VMEM(packed, jnp.float32),
        ],
        compiler_params=pltpu.CompilerParams(vmem_limit_bytes=VMEM_LIMIT),
        cost_estimate=pl.CostEstimate(
            flops=16 * count * count * rows, bytes_accessed=10 * count * rows, transcendentals=0
        ),
    )(core, vectors, kin, vector_sums, pot, precond)


def solve_kernel(
    full_rows, reps, core_ref, mine_ref, other_ref, vectors_ref, image_ref, precond_ref,
    out_ref, rayleigh_ref, mix_ref, sums_ref
):
    count, width = image_ref.shape
    vecs = count // reps

    @pl.when(pl.program_id(0) == 0)
    def _():
        size = mine_ref.shape[0]
        core = core_ref[0]
        sums_ref[pl.ds(pl.multiple_of(core * size, 8), size), :] = mine_ref[...]
        sums_ref[pl.ds(pl.multiple_of((1 - core) * size, 8), size), :] = other_ref[...]
        row, column = iota((count, count), 0), iota((count, count), 1)
        shared = sums_ref[0:count, 0:count]
        shared_t = shared.T
        own = jnp.where(row <= column, shared, shared_t)
        vector = jnp.where(row <= column, shared_t, shared)
        diagonal = sums_ref[2 * count + vecs:2 * count + vecs + 1, 0:count]
        vector = jnp.where(row == column, diagonal, vector)
        turned = sums_ref[count:2 * count, 0:count] / full_rows
        rayleigh = turned.T
        rayleigh_ref[...] = rayleigh
        third = jnp.concatenate([
            sums_ref[2 * count:2 * count + vecs, b * PAD:(b + 1) * PAD] for b in range(reps)
        ], axis=0)
        mixed = jnp.concatenate(
            [sums_ref[0:count, count:], sums_ref[count:2 * count, count:], third], axis=1
        )
        cross = dot_exact(mixed, rayleigh)
        last = dot_exact(turned, dot_exact(vector, rayleigh))
        gram = (own - cross - cross.T + last) / full_rows
        pad = jnp.zeros((count, LANES - count), jnp.float32)
        row, column = iota((count, LANES), 0), iota((count, LANES), 1)
        left = jnp.concatenate([gram, pad], axis=1)
        right = jnp.where(row == column, 1.0, 0.0)
        for j in range(0, count, 2):
            first, second = left[j:j + 1, :], left[j + 1:j + 2, :]
            a, b, c = first[:, j:j + 1], first[:, j + 1:j + 2], second[:, j + 1:j + 2]
            over = 1.0 / (a * c - b * b)
            below = row[:, 0:1] > j + 1
            one, two = left[:, j:j + 1], left[:, j + 1:j + 2]
            ratio_one = jnp.where(below, (one * c - two * b) * over, 0.0)
            ratio_two = jnp.where(below, (two * a - one * b) * over, 0.0)
            left = left - (ratio_one * first + ratio_two * second)
            right = right - (ratio_one * right[j:j + 1, :] + ratio_two * right[j + 1:j + 2, :])
        diagonal = jnp.sum(jnp.where(row == column, left, 0.0), axis=1, keepdims=True)
        beside = jnp.sum(jnp.where(row == column + 1, left, 0.0), axis=1, keepdims=True)
        diagonal = jnp.broadcast_to(diagonal, left.shape)
        ratio = jnp.where(row % 2 == 1, beside / pltpu.roll(diagonal, 1, 0), 0.0)
        right = right - ratio * pltpu.roll(right, 1, 0)
        inverse = (right * lax.rsqrt(diagonal - ratio * beside))[:, 0:count]
        parts = three_parts(inverse) + three_parts(-dot_exact(inverse, turned))
        for k in range(3):
            mix_ref[k * count:(k + 1) * count, 0:count] = parts[k]
            mix_ref[k * count:(k + 1) * count, count:2 * count] = parts[3 + k]

    both = jnp.concatenate([image_ref[...], vectors_ref[...]], axis=0)
    chunk = 512
    for s in range(0, width, chunk):
        parts = jnp.dot(mix_ref[...], both[:, s:s + chunk], preferred_element_type=jnp.float32)
        total = (parts[2 * count:] + parts[count:2 * count]) + parts[0:count]
        out_ref[:, 0, s:s + chunk] = total * precond_ref[0:1, s:s + chunk]


def solved_of(core, mine, other, vectors, image, precond, full_rows, reps, steps):
    count, rows = image.shape
    width = rows // steps
    return pl.pallas_call(
        functools.partial(solve_kernel, full_rows, reps),
        grid=(steps,),
        out_shape=(
            jax.ShapeDtypeStruct((count, 1, rows), jnp.float32),
            jax.ShapeDtypeStruct((count, count), jnp.float32),
        ),
        in_specs=[
            SCALARS,
            pl.BlockSpec(mine.shape, lambda i: (0, 0)),
            pl.BlockSpec(mine.shape, lambda i: (0, 0)),
            pl.BlockSpec((count, width), lambda i: (0, i)),
            pl.BlockSpec((count, width), lambda i: (0, i)),
            pl.BlockSpec((1, width), lambda i: (0, i)),
        ],
        out_specs=(
            pl.BlockSpec((count, 1, width), lambda i: (0, 0, i)),
            pl.BlockSpec((count, count), lambda i: (0, 0)),
        ),
        scratch_shapes=[
            pltpu.VMEM((3 * count, 2 * count), jnp.bfloat16),
            pltpu.VMEM((2 * mine.shape[0], LANES), jnp.float32),
        ],
        compiler_params=pltpu.CompilerParams(vmem_limit_bytes=VMEM_LIMIT),
        cost_estimate=pl.CostEstimate(
            flops=12 * count * count * rows, bytes_accessed=8 * count * rows, transcendentals=0
        ),
    )(core, mine, other, vectors, image, precond)


def sum_over_devices(keep, give):
    def turned(x, axis, stride, shift):
        pairs = []
        for i in range(lax.axis_size(axis)):
            digit = (i // stride) % 4
            pairs.append((i, i + ((digit + shift) % 4 - digit) * stride))
        return lax.ppermute(x, axis, pairs)

    swap = [(i, i ^ 1) for i in range(lax.axis_size("row"))]
    x = keep + lax.ppermute(give, "row", swap)
    for axis, stride in (("rep", 1), ("row", 8), ("row", 2)):
        up, down, across = (turned(x, axis, stride, shift) for shift in (1, 3, 2))
        x = (x + across) + (up + down)
    return x, lax.ppermute(x, "row", swap)


def body(
    basis_vecs, potential, surface, grid_perm, kinetic, couplings, coupling_coefficient, precond
):
    vecs, rows = basis_vecs.shape
    pieces = lax.axis_size("row")
    reps = lax.axis_size("rep")
    width = rows // pieces
    blocks = rows // BLK
    edge = HB * BLK
    forward = [(i, i + 1) for i in range(pieces - 1)]
    backward = [(i + 1, i) for i in range(pieces - 1)]
    low = lax.ppermute(basis_vecs[:, rows - edge:], "row", forward)
    high = lax.ppermute(basis_vecs[:, :edge], "row", backward)
    by_piece = basis_vecs.reshape(vecs, pieces, width).transpose(1, 0, 2)
    by_piece, low, high, perm = lax.optimization_barrier((by_piece, low, high, grid_perm))
    arrived = lax.all_to_all(by_piece, "row", split_axis=0, concat_axis=0, tiled=True)
    columns = couplings[:, 1] - (lax.axis_index("row") * blocks - HB)
    rep = lax.axis_index("rep").reshape(1)
    core = (lax.axis_index("row") % 2).reshape(1)
    parts = source_of(rep, basis_vecs, low, high, columns, coupling_coefficient, reps)
    parts = [
        part if s == 0 else lax.ppermute(part, "rep", [(i, (i - s) % reps) for i in range(reps)])
        for s, part in enumerate(parts)
    ]
    out, back = index_streams(perm, reps)
    restored = surface_pass(arrived, out, back, potential, surface, reps)
    pot = lax.all_to_all(restored, ("rep", "row"), split_axis=0, concat_axis=0, tiled=True)
    pot = pot.reshape(reps, pieces, vecs, width // reps)
    scale = precond.reshape(1, -1)
    vectors, kin, vector_sums = vectors_of(rep, parts, kinetic, scale, 8)
    image, keep, give = image_of(core, vectors, kin, vector_sums, pot, scale, 8)
    mine, other = sum_over_devices(keep, give)
    solved, rayleigh = solved_of(
        core, mine, other, vectors, image, scale, float(rows * pieces), reps, 8
    )
    return (solved.reshape(reps * vecs, 1, 1, -1), rayleigh)


def solution(mesh):
    in_specs = (
        P("rep", "row"),
        P("row"),
        P(),
        P("row"),
        P(),
        P("row", None),
        P("row"),
        P("row", "rep", None),
    )
    out_specs = (P(None, "row", "rep", None), P())
    return jax.shard_map(body, mesh=mesh, in_specs=in_specs, out_specs=out_specs, check_vma=False)
```

```python
import functools

import jax
import jax.numpy as jnp
from jax import lax
from jax.experimental import pallas as pl
from jax.experimental.pallas import tpu as pltpu
from jax.sharding import PartitionSpec as P

HB = 2
COUPLINGS_PER_ROW = 3
BLK = 256
PAD = 32
GROUPS = 4
LANES = 128
SPAN = GROUPS * BLK
VMEM_LIMIT = 60 * 2**20
NT = (((1,), (1,)), ((), ()))
WHOLE = pl.BlockSpec(memory_space=pltpu.VMEM)
SCALARS = pl.BlockSpec(memory_space=pltpu.SMEM)


def dot_nt(a, b):
    return lax.dot_general(a, b, NT, preferred_element_type=jnp.float32)


def dot_exact(a, b):
    return jnp.dot(a, b, precision=lax.Precision.HIGHEST, preferred_element_type=jnp.float32)


def iota(shape, dim):
    return lax.broadcasted_iota(jnp.int32, shape, dim)


def three_parts(x):
    high = x.astype(jnp.bfloat16)
    rest = x - high.astype(jnp.float32)
    middle = rest.astype(jnp.bfloat16)
    low = (rest - middle.astype(jnp.float32)).astype(jnp.bfloat16)
    return [high, middle, low]


def inverse_kernel(reps, perm_ref, power_ref, out_ref, back_ref, acc_ref):
    blocks = perm_ref.shape[0]
    half = blocks // 2
    step = 4
    rows = iota((BLK, BLK), 0)
    lane = iota((1, BLK), 1)
    code = jnp.where(lane < 128, lane + 128, -lane).astype(jnp.float32)

    for part in range(2):
        mine = slice(part * BLK, (part + 1) * BLK)
        acc_ref[mine, :] = jnp.zeros((BLK, BLK), jnp.float32)

        @pl.loop(0, half // 8)
        def _(i):
            tile = perm_ref[pl.ds(pl.multiple_of(part * half + i * 8, 8), 8), :]
            high = tile >> 8
            low = tile & 255
            for first in range(0, 8, step):
                left, right = [], []
                for k in range(first, first + step):
                    value = code * power_ref[i * 8 + k]
                    left.append(
                        jnp.where(rows == high[k:k + 1, :], value, 0.0).astype(jnp.bfloat16)
                    )
                    right.append(
                        jnp.where(rows == low[k:k + 1, :], 1.0, 0.0).astype(jnp.bfloat16)
                    )
                acc_ref[mine, :] += dot_nt(
                    jnp.concatenate(left, axis=1), jnp.concatenate(right, axis=1)
                )

    for r in range(0, BLK, 32):
        late = acc_ref[BLK + r:BLK + r + 32, :]
        held = acc_ref[r:r + 32, :] + late
        size = jnp.abs(held)
        number = jnp.where(late != 0.0, 32768.0, 0.0) + jnp.where(held < 0.0, 128.0, 0.0)
        for bit in (64, 32, 16, 8, 4, 2, 1):
            above = size >= 2.0 ** (bit - 57)
            size = jnp.where(above, size * 2.0 ** -bit, size)
            number = number + jnp.where(above, bit * 256.0, 0.0)
        acc_ref[r:r + 32, :] = number + (size * 2.0 ** 64 - 128.0)

    per_rep = 8 // reps
    for d in range(blocks // 8):
        tile = acc_ref[d * 8:(d + 1) * 8, :]
        for b in range(reps):
            start = BLK + b * (blocks // reps) + d * per_rep
            acc_ref[start:start + per_rep, :] = tile[b * per_rep:(b + 1) * per_rep, :]
    for k in range(2):
        out_ref[k * BLK:(k + 1) * BLK, :] = perm_ref[k * half:(k + 1) * half, :].T
        back_ref[k * BLK:(k + 1) * BLK, :] = acc_ref[
            BLK + k * half:BLK + (k + 1) * half, :
        ].T.astype(jnp.int32)


def index_streams(perm, reps):
    blocks = perm.shape[0] // BLK
    streams = jax.ShapeDtypeStruct((2 * BLK, blocks // 2), jnp.int32)
    powers = jnp.asarray([2.0 ** (k - 64) for k in range(blocks // 2)], jnp.float32)
    out, back = pl.pallas_call(
        functools.partial(inverse_kernel, reps),
        out_shape=(streams, streams),
        in_specs=[WHOLE, SCALARS],
        out_specs=(WHOLE, WHOLE),
        scratch_shapes=[pltpu.VMEM((2 * BLK, BLK), jnp.float32)],
        compiler_params=pltpu.CompilerParams(vmem_limit_bytes=VMEM_LIMIT),
        cost_estimate=pl.CostEstimate(
            flops=2 * BLK * BLK * blocks * BLK, bytes_accessed=8 * blocks * BLK, transcendentals=0
        ),
    )(perm.reshape(blocks, BLK), powers)
    return out.reshape(-1), back.reshape(-1)


def stream(index_ref, streams, sem, table_ref, rows_refs, work):
    sublane = iota((8, LANES), 0)
    size = streams[0].shape[0]
    half = size // 8
    count = half // 2
    copies = [
        pltpu.make_async_copy(index_ref.at[pl.ds(k * size, size)], held, sem.at[k])
        for k, held in enumerate(streams)
    ]

    def gather(i, rows_ref):
        def tile(held, places):
            value = None
            for t in range(8):
                row = jnp.broadcast_to(table_ref[pl.ds(held[places[t]], 1), :], (8, LANES))
                value = row if value is None else jnp.where(sublane == t, row, value)
            return value

        for part in range(2):
            places = [t * half + 2 * i + part for t in range(8)]
            for k in range(0, len(streams), 2):
                both = jnp.concatenate([tile(held, places) for held in streams[k:k + 2]], axis=0)
                first = part * len(streams) * 8 + k * 8
                rows_ref[first:first + 16, :] = both.astype(jnp.bfloat16)

    def begin():
        for copy in copies:
            copy.start()

    def run():
        for copy in copies:
            copy.wait()
        def gather_pair(i, rows_ref):
            for k in range(2):
                gather(2 * jnp.minimum(i, count // 2 - 1) + k, rows_ref.at[pl.ds(k * SPAN, SPAN), :])

        gather_pair(0, rows_refs[0])

        @pl.loop(0, count // 4)
        def _(j):
            for s in range(2):
                i = j * 2 + s
                gather_pair(i + 1, rows_refs[(s + 1) % 2])
                work(i, rows_refs[s % 2])

    return begin, run


def blocks_of(i, blocks):
    return [2 * i, 2 * i + blocks // 2, 2 * i + 1, 2 * i + 1 + blocks // 2]


def surface_kernel(
    arrived_ref, perm_ref, back_ref, pot_ref, surf_ref, out_ref,
    x_ref, x_sem, table_ref, packed_ref, even_ref, odd_ref, *rest
):
    streams, sem = rest[:-1], rest[-1]
    arrival = pltpu.make_async_copy(arrived_ref, x_ref, x_sem)
    arrival.start()
    pieces, vecs, width = x_ref.shape
    points = table_ref.shape[0]
    per_group = pieces // GROUPS
    group_rows = points // GROUPS
    row, column = iota((LANES, GROUPS * LANES), 0), iota((LANES, GROUPS * LANES), 1)
    fold = jnp.where(
        (row // PAD == column // LANES) & (row % PAD == column % PAD), 1.0, 0.0
    ).astype(jnp.bfloat16)
    unit = jnp.where(iota((BLK, BLK), 0) == iota((BLK, BLK), 1), 1.0, 0.0).astype(jnp.bfloat16)
    lane_group = iota((BLK, LANES), 1) // PAD
    count = points // SPAN
    blocks = points // BLK

    def folded(rows_ref, k):
        wide = jnp.concatenate([
            rows_ref[k * SPAN + q * BLK:k * SPAN + (q + 1) * BLK, :] for q in range(GROUPS)
        ], axis=1)
        return dot_nt(fold, wide).astype(jnp.bfloat16)

    def spread(rows, starts):
        for q in range(GROUPS):
            table_ref[pl.ds(pl.multiple_of(starts[q], BLK), BLK), :] = jnp.where(
                lane_group == q, rows, 0.0
            )

    def to_grid_and_back(i, rows_ref):
        values = jnp.concatenate([folded(rows_ref, k) for k in range(2)], axis=0)
        projected = jnp.dot(values, surf_ref[...], preferred_element_type=jnp.float32)
        held = blocks_of(2 * i, blocks) + blocks_of(2 * i + 1, blocks)
        weighted = jnp.concatenate([
            projected[q * PAD:(q + 1) * PAD] * pot_ref[pl.ds(block, 1), :]
            for q, block in enumerate(held)
        ], axis=0).astype(jnp.bfloat16)
        returned = dot_nt(surf_ref[...], weighted).astype(jnp.bfloat16).astype(jnp.float32)
        for k in range(2):
            start = pl.multiple_of((2 * i + k) * BLK, BLK)
            packed_ref[pl.ds(start, BLK), :] = returned[:, k * LANES:(k + 1) * LANES]

    def to_basis(i, rows_ref):
        per_piece = out_ref.shape[2] // BLK
        for k in range(2):
            values = folded(rows_ref, k)
            for q in range(GROUPS):
                at = (q // per_piece) * BLK
                piece = 2 * i + k + (q % per_piece) * (out_ref.shape[0] // per_piece)
                out_ref[piece, :, at:at + BLK] = values[q * PAD:q * PAD + vecs]

    begin, run = stream(perm_ref, streams, sem, table_ref, (even_ref, odd_ref), to_grid_and_back)
    begin()
    arrival.wait()
    chunk = 512

    @pl.loop(0, per_group)
    def _(d):
        for c in range(0, width, chunk):
            parts = []
            for q in range(GROUPS):
                parts.append(x_ref[q * per_group + d, :, c:c + chunk].astype(jnp.float32))
                parts.append(jnp.zeros((PAD - vecs, chunk), jnp.float32))
            stacked = jnp.concatenate(parts, axis=0).astype(jnp.bfloat16)
            for h in range(0, chunk, BLK):
                rows = dot_nt(unit, stacked[:, h:h + BLK])
                spread(rows, [q * group_rows + d * width + c + h for q in range(GROUPS)])

    run()
    begin, run = stream(back_ref, streams, sem, table_ref, (even_ref, odd_ref), to_basis)
    begin()

    @pl.loop(0, count)
    def _(i):
        rows = packed_ref[pl.ds(pl.multiple_of(i * BLK, BLK), BLK), :]
        spread(rows, [block * BLK for block in blocks_of(i, blocks)])

    run()


def surface_pass(arrived, perm, back, potential, surface, reps):
    pieces, vecs, width = arrived.shape
    points = perm.shape[0]
    return pl.pallas_call(
        surface_kernel,
        out_shape=jax.ShapeDtypeStruct((pieces * reps, vecs, width // reps), jnp.bfloat16),
        in_specs=[pl.BlockSpec(memory_space=pl.ANY)] + [WHOLE] * 4,
        out_specs=WHOLE,
        scratch_shapes=[
            pltpu.VMEM(arrived.shape, jnp.bfloat16),
            pltpu.SemaphoreType.DMA,
            pltpu.VMEM((points, LANES), jnp.float32),
            pltpu.VMEM((points // GROUPS, LANES), jnp.float32),
            pltpu.VMEM((2 * SPAN, LANES), jnp.bfloat16),
            pltpu.VMEM((2 * SPAN, LANES), jnp.bfloat16),
        ] + [pltpu.SMEM((4 * BLK,), jnp.int32)] * 64 + [pltpu.SemaphoreType.DMA((64,))],
        compiler_params=pltpu.CompilerParams(vmem_limit_bytes=VMEM_LIMIT),
        cost_estimate=pl.CostEstimate(
            flops=4 * vecs * points * BLK, bytes_accessed=300_000_000, transcendentals=0
        ),
    )(arrived, perm, back, potential.reshape(-1, BLK), surface)


def source_kernel(vecs_ref, low_ref, high_ref, column_ref, weight_ref, out_ref, wide_ref):
    reps = out_ref.shape[0]
    edge = low_ref.shape[1]
    rows = vecs_ref.shape[1]
    blocks = rows // BLK
    piece_blocks = out_ref.shape[3] * reps // (blocks * BLK)
    wide_ref[:, 0:edge] = low_ref[...]
    wide_ref[:, edge + rows:] = high_ref[...]
    per_piece = 8
    per_rep = per_piece // reps

    @pl.loop(0, blocks // per_piece)
    def _(j):
        start = pl.multiple_of(j * per_piece * BLK, per_piece * BLK)
        wide_ref[:, pl.ds(edge + start, per_piece * BLK)] = vecs_ref[:, pl.ds(start, per_piece * BLK)]

    @pl.loop(0, blocks // per_piece)
    def _(j):
        for k in range(per_piece):
            a = j * per_piece + k
            total = None
            for m in range(COUPLINGS_PER_ROW):
                c = a * COUPLINGS_PER_ROW + m
                at = pl.multiple_of(column_ref[c] * BLK, BLK)
                term = wide_ref[:, pl.ds(at, BLK)].astype(jnp.float32) * weight_ref[c]
                total = term if total is None else total + term
            to = pl.ds(pl.multiple_of(j * per_rep * BLK, per_rep * BLK) + (k % per_rep) * BLK, BLK)
            here = pl.multiple_of(a * BLK, BLK)
            out_ref[k // per_rep, 0, :, to] = vecs_ref[:, pl.ds(here, BLK)]
            out_ref[k // per_rep, 1, :, to] = total.astype(jnp.bfloat16)


def source_of(basis_vecs, low, high, columns, weights, reps):
    vecs, rows = basis_vecs.shape
    return pl.pallas_call(
        source_kernel,
        out_shape=jax.ShapeDtypeStruct((reps, 2, vecs, rows // reps), jnp.bfloat16),
        in_specs=[WHOLE, WHOLE, WHOLE, SCALARS, SCALARS],
        out_specs=WHOLE,
        scratch_shapes=[pltpu.VMEM((vecs, rows + 2 * low.shape[1]), jnp.bfloat16)],
        compiler_params=pltpu.CompilerParams(vmem_limit_bytes=VMEM_LIMIT),
        cost_estimate=pl.CostEstimate(
            flops=6 * vecs * rows, bytes_accessed=12 * vecs * rows, transcendentals=0
        ),
    )(basis_vecs, low, high, columns, weights)


def vector_kernel(
    moved_ref, kinetic_ref, precond_ref, vectors_ref, kin_ref, sums_ref, total_ref
):
    step = pl.program_id(0)
    reps, _, vecs, width = moved_ref.shape
    count = reps * vecs

    @pl.when(step == 0)
    def _():
        total_ref[...] = jnp.zeros_like(total_ref)

    def ordered(k):
        return jnp.concatenate([moved_ref[b, k].astype(jnp.float32) for b in range(reps)], axis=0)

    vectors = ordered(0)
    vectors_16 = vectors.astype(jnp.bfloat16)
    vectors_ref[...] = vectors_16
    scale = precond_ref[...]
    left = jnp.concatenate(three_parts(vectors * (scale * scale)), axis=0)
    total_ref[...] += dot_nt(left, vectors_16)
    source = ordered(1).astype(jnp.bfloat16)
    blocks = [source[:, h:h + BLK] for h in range(0, width, BLK)]
    kin = jnp.dot(jnp.concatenate(blocks, axis=0), kinetic_ref[...], preferred_element_type=jnp.float32)
    for h in range(width // BLK):
        kin_ref[:, h * BLK:(h + 1) * BLK] = kin[h * count:(h + 1) * count]

    @pl.when(step == pl.num_programs(0) - 1)
    def _():
        sums_ref[...] = (
            total_ref[0:count] + total_ref[count:2 * count] + total_ref[2 * count:3 * count]
        )


def vectors_of(moved, kinetic, precond, steps):
    reps, _, vecs, rows = moved.shape
    width = rows // steps
    count = reps * vecs
    return pl.pallas_call(
        vector_kernel,
        grid=(steps,),
        out_shape=(
            jax.ShapeDtypeStruct((count, rows), jnp.bfloat16),
            jax.ShapeDtypeStruct((count, rows), jnp.float32),
            jax.ShapeDtypeStruct((count, count), jnp.float32),
        ),
        in_specs=[
            pl.BlockSpec((reps, 2, vecs, width), lambda i: (0, 0, 0, i)),
            pl.BlockSpec((BLK, BLK), lambda i: (0, 0)),
            pl.BlockSpec((1, width), lambda i: (0, i)),
        ],
        out_specs=(
            pl.BlockSpec((count, width), lambda i: (0, i)),
            pl.BlockSpec((count, width), lambda i: (0, i)),
            pl.BlockSpec((count, count), lambda i: (0, 0)),
        ),
        scratch_shapes=[pltpu.VMEM((3 * count, count), jnp.float32)],
        compiler_params=pltpu.CompilerParams(vmem_limit_bytes=VMEM_LIMIT),
        cost_estimate=pl.CostEstimate(
            flops=12 * count * count * rows, bytes_accessed=8 * count * rows, transcendentals=0
        ),
    )(moved, kinetic, precond)


def image_kernel(
    core_ref, vectors_ref, kin_ref, vector_sums_ref, pot_ref, precond_ref,
    image_ref, keep_ref, give_ref, total_ref, sums_ref
):
    step = pl.program_id(0)
    count, width = vectors_ref.shape
    reps, _, vecs, segment = pot_ref.shape

    @pl.when(step == 0)
    def _():
        total_ref[...] = jnp.zeros_like(total_ref)

    for s in range(width // segment):
        at = slice(s * segment, (s + 1) * segment)
        pot = jnp.concatenate([pot_ref[b, s].astype(jnp.float32) for b in range(reps)], axis=0)
        image = (kin_ref[:, at] + pot).astype(jnp.bfloat16)
        image_ref[:, at] = image
        scale = precond_ref[0:1, at]
        scaled = three_parts(image.astype(jnp.float32) * (scale * scale))
        left = jnp.concatenate(scaled + [image], axis=0)
        total_ref[...] += dot_nt(left, jnp.concatenate([image, vectors_ref[:, at]], axis=0))

    @pl.when(step == pl.num_programs(0) - 1)
    def _():
        scaled = total_ref[0:count] + total_ref[count:2 * count] + total_ref[2 * count:3 * count]
        own, cross = scaled[:, 0:count], scaled[:, count:2 * count]
        plain = total_ref[3 * count:4 * count, count:2 * count]
        vector = vector_sums_ref[...]
        row, column = iota((count, count), 0), iota((count, count), 1)
        own = jnp.where(row <= column, own, vector)
        diagonal = jnp.sum(jnp.where(row == column, vector, 0.0), axis=0, keepdims=True)
        sums_ref[0:count, :] = jnp.concatenate([own, cross[:, 0:PAD]], axis=1)
        sums_ref[count:2 * count, :] = jnp.concatenate([plain, cross[:, PAD:2 * PAD]], axis=1)
        sums_ref[2 * count:2 * count + vecs, :] = jnp.concatenate(
            [cross[b * vecs:(b + 1) * vecs, 2 * PAD:3 * PAD] for b in range(reps)], axis=1
        )
        sums_ref[2 * count + vecs:, :] = jnp.broadcast_to(
            jnp.concatenate([diagonal, jnp.zeros((1, PAD), jnp.float32)], axis=1), (8, LANES)
        )
        size = keep_ref.shape[0]
        core = core_ref[0]
        keep_ref[...] = sums_ref[pl.ds(pl.multiple_of(core * size, 8), size), :]
        give_ref[...] = sums_ref[pl.ds(pl.multiple_of((1 - core) * size, 8), size), :]


def image_of(core, vectors, kin, vector_sums, pot, precond, steps):
    count, rows = vectors.shape
    reps, pieces, vecs, segment = pot.shape
    width = rows // steps
    packed = (2 * count + vecs + 8, LANES)
    half = (packed[0] // 2, LANES)
    return pl.pallas_call(
        image_kernel,
        grid=(steps,),
        out_shape=(
            jax.ShapeDtypeStruct((count, rows), jnp.bfloat16),
            jax.ShapeDtypeStruct(half, jnp.float32),
            jax.ShapeDtypeStruct(half, jnp.float32),
        ),
        in_specs=[
            SCALARS,
            pl.BlockSpec((count, width), lambda i: (0, i)),
            pl.BlockSpec((count, width), lambda i: (0, i)),
            pl.BlockSpec((count, count), lambda i: (0, 0)),
            pl.BlockSpec((reps, pieces // steps, vecs, segment), lambda i: (0, i, 0, 0)),
            pl.BlockSpec((1, width), lambda i: (0, i)),
        ],
        out_specs=(
            pl.BlockSpec((count, width), lambda i: (0, i)),
            pl.BlockSpec(half, lambda i: (0, 0)),
            pl.BlockSpec(half, lambda i: (0, 0)),
        ),
        scratch_shapes=[
            pltpu.VMEM((4 * count, 2 * count), jnp.float32),
            pltpu.VMEM(packed, jnp.float32),
        ],
        compiler_params=pltpu.CompilerParams(vmem_limit_bytes=VMEM_LIMIT),
        cost_estimate=pl.CostEstimate(
            flops=16 * count * count * rows, bytes_accessed=10 * count * rows, transcendentals=0
        ),
    )(core, vectors, kin, vector_sums, pot, precond)


def solve_kernel(
    full_rows, reps, core_ref, mine_ref, other_ref, vectors_ref, image_ref, precond_ref,
    out_ref, rayleigh_ref, mix_ref, sums_ref
):
    count, width = image_ref.shape
    vecs = count // reps

    @pl.when(pl.program_id(0) == 0)
    def _():
        size = mine_ref.shape[0]
        core = core_ref[0]
        sums_ref[pl.ds(pl.multiple_of(core * size, 8), size), :] = mine_ref[...]
        sums_ref[pl.ds(pl.multiple_of((1 - core) * size, 8), size), :] = other_ref[...]
        row, column = iota((count, count), 0), iota((count, count), 1)
        shared = sums_ref[0:count, 0:count]
        shared_t = shared.T
        own = jnp.where(row <= column, shared, shared_t)
        vector = jnp.where(row <= column, shared_t, shared)
        diagonal = sums_ref[2 * count + vecs:2 * count + vecs + 1, 0:count]
        vector = jnp.where(row == column, diagonal, vector)
        turned = sums_ref[count:2 * count, 0:count] / full_rows
        rayleigh = turned.T
        rayleigh_ref[...] = rayleigh
        third = jnp.concatenate([
            sums_ref[2 * count:2 * count + vecs, b * PAD:(b + 1) * PAD] for b in range(reps)
        ], axis=0)
        mixed = jnp.concatenate(
            [sums_ref[0:count, count:], sums_ref[count:2 * count, count:], third], axis=1
        )
        cross = dot_exact(mixed, rayleigh)
        last = dot_exact(turned, dot_exact(vector, rayleigh))
        gram = (own - cross - cross.T + last) / full_rows
        pad = jnp.zeros((8, LANES - count), jnp.float32)
        row, column = iota((8, LANES), 0), iota((8, LANES), 1)
        left, right = [], []
        for k in range(0, count, 8):
            left.append(jnp.concatenate([gram[k:k + 8, :], pad], axis=1))
            right.append(jnp.where(row + k == column, 1.0, 0.0))
        for j in range(count):
            own, at = j // 8, j % 8
            over = 1.0 / left[own][at:at + 1, j:j + 1]
            pivot_left = left[own][at:at + 1, :] * over
            pivot_right = right[own][at:at + 1, :] * over
            for k in range(own, count // 8):
                ratio = left[k][:, j:j + 1]
                if k == own:
                    ratio = jnp.where(row[:, 0:1] > at, ratio, 0.0)
                left[k] = left[k] - ratio * pivot_left
                right[k] = right[k] - ratio * pivot_right
        scaled = []
        for k in range(count // 8):
            pivots = jnp.where(row + k * 8 == column, left[k], 0.0)
            scaled.append(right[k] * lax.rsqrt(jnp.sum(pivots, axis=1, keepdims=True)))
        inverse = jnp.concatenate(scaled, axis=0)[:, 0:count]
        parts = three_parts(inverse) + three_parts(-dot_exact(inverse, turned))
        for k in range(3):
            mix_ref[k * count:(k + 1) * count, 0:count] = parts[k]
            mix_ref[k * count:(k + 1) * count, count:2 * count] = parts[3 + k]

    both = jnp.concatenate([image_ref[...], vectors_ref[...]], axis=0)
    chunk = 512
    for s in range(0, width, chunk):
        parts = jnp.dot(mix_ref[...], both[:, s:s + chunk], preferred_element_type=jnp.float32)
        total = (parts[2 * count:] + parts[count:2 * count]) + parts[0:count]
        out_ref[:, 0, s:s + chunk] = total * precond_ref[0:1, s:s + chunk]


def solved_of(core, mine, other, vectors, image, precond, full_rows, reps, steps):
    count, rows = image.shape
    width = rows // steps
    return pl.pallas_call(
        functools.partial(solve_kernel, full_rows, reps),
        grid=(steps,),
        out_shape=(
            jax.ShapeDtypeStruct((count, 1, rows), jnp.float32),
            jax.ShapeDtypeStruct((count, count), jnp.float32),
        ),
        in_specs=[
            SCALARS,
            pl.BlockSpec(mine.shape, lambda i: (0, 0)),
            pl.BlockSpec(mine.shape, lambda i: (0, 0)),
            pl.BlockSpec((count, width), lambda i: (0, i)),
            pl.BlockSpec((count, width), lambda i: (0, i)),
            pl.BlockSpec((1, width), lambda i: (0, i)),
        ],
        out_specs=(
            pl.BlockSpec((count, 1, width), lambda i: (0, 0, i)),
            pl.BlockSpec((count, count), lambda i: (0, 0)),
        ),
        scratch_shapes=[
            pltpu.VMEM((3 * count, 2 * count), jnp.bfloat16),
            pltpu.VMEM((2 * mine.shape[0], LANES), jnp.float32),
        ],
        compiler_params=pltpu.CompilerParams(vmem_limit_bytes=VMEM_LIMIT),
        cost_estimate=pl.CostEstimate(
            flops=12 * count * count * rows, bytes_accessed=8 * count * rows, transcendentals=0
        ),
    )(core, mine, other, vectors, image, precond)


def sum_over_devices(keep, give):
    def turned(x, axis, stride, shift):
        pairs = []
        for i in range(lax.axis_size(axis)):
            digit = (i // stride) % 4
            pairs.append((i, i + ((digit + shift) % 4 - digit) * stride))
        return lax.ppermute(x, axis, pairs)

    swap = [(i, i ^ 1) for i in range(lax.axis_size("row"))]
    x = keep + lax.ppermute(give, "row", swap)
    for axis, stride in (("rep", 1), ("row", 8), ("row", 2)):
        up, down, across = (turned(x, axis, stride, shift) for shift in (1, 3, 2))
        x = (x + across) + (up + down)
    return x, lax.ppermute(x, "row", swap)


def body(
    basis_vecs, potential, surface, grid_perm, kinetic, couplings, coupling_coefficient, precond
):
    vecs, rows = basis_vecs.shape
    pieces = lax.axis_size("row")
    reps = lax.axis_size("rep")
    width = rows // pieces
    blocks = rows // BLK
    edge = HB * BLK
    forward = [(i, i + 1) for i in range(pieces - 1)]
    backward = [(i + 1, i) for i in range(pieces - 1)]
    low = lax.ppermute(basis_vecs[:, rows - edge:], "row", forward)
    high = lax.ppermute(basis_vecs[:, :edge], "row", backward)
    by_piece = basis_vecs.reshape(vecs, pieces, width).transpose(1, 0, 2)
    arrived = lax.all_to_all(by_piece, "row", split_axis=0, concat_axis=0, tiled=True)
    columns = couplings[:, 1] - (lax.axis_index("row") * blocks - HB)
    by_rep = source_of(basis_vecs, low, high, columns, coupling_coefficient, reps)
    out, back = index_streams(grid_perm, reps)
    by_rep, out, back = lax.optimization_barrier((by_rep, out, back))
    moved = lax.all_to_all(by_rep, "rep", split_axis=0, concat_axis=0, tiled=True)
    restored = surface_pass(arrived, out, back, potential, surface, reps)
    restored, moved = lax.optimization_barrier((restored, moved))
    pot = lax.all_to_all(restored, ("rep", "row"), split_axis=0, concat_axis=0, tiled=True)
    pot = pot.reshape(reps, pieces, vecs, width // reps)
    scale = precond.reshape(1, -1)
    core = (lax.axis_index("row") % 2).reshape(1)
    vectors, kin, vector_sums = vectors_of(moved, kinetic, scale, 4)
    image, keep, give = image_of(core, vectors, kin, vector_sums, pot, scale, 4)
    mine, other = sum_over_devices(keep, give)
    solved, rayleigh = solved_of(
        core, mine, other, vectors, image, scale, float(rows * pieces), reps, 4
    )
    return (solved.reshape(reps * vecs, 1, 1, -1), rayleigh)


def solution(mesh):
    in_specs = (
        P("rep", "row"),
        P("row"),
        P(),
        P("row"),
        P(),
        P("row", None),
        P("row"),
        P("row", "rep", None),
    )
    out_specs = (P(None, "row", "rep", None), P())
    return jax.shard_map(body, mesh=mesh, in_specs=in_specs, out_specs=out_specs, check_vma=False)
```

```python
import functools

import jax
import jax.numpy as jnp
from jax import lax
from jax.experimental import pallas as pl
from jax.experimental.pallas import tpu as pltpu
from jax.sharding import PartitionSpec as P

HB = 2
COUPLINGS_PER_ROW = 3
BLK = 256
PAD = 32
GROUPS = 4
LANES = 128
SPAN = GROUPS * BLK
VMEM_LIMIT = 62 * 2**20
NT = (((1,), (1,)), ((), ()))
WHOLE = pl.BlockSpec(memory_space=pltpu.VMEM)
SCALARS = pl.BlockSpec(memory_space=pltpu.SMEM)


def dot_nt(a, b):
    return lax.dot_general(a, b, NT, preferred_element_type=jnp.float32)


def dot_exact(a, b):
    return jnp.dot(a, b, precision=lax.Precision.HIGHEST, preferred_element_type=jnp.float32)


def iota(shape, dim):
    return lax.broadcasted_iota(jnp.int32, shape, dim)


def three_parts(x):
    high = x.astype(jnp.bfloat16)
    rest = x - high.astype(jnp.float32)
    middle = rest.astype(jnp.bfloat16)
    low = (rest - middle.astype(jnp.float32)).astype(jnp.bfloat16)
    return [high, middle, low]


def inverse_kernel(reps, perm_ref, power_ref, out_ref, back_ref, acc_ref):
    blocks = perm_ref.shape[0]
    half = blocks // 2
    step = 4
    rows = iota((BLK, BLK), 0)
    lane = iota((1, BLK), 1)
    code = jnp.where(lane < 128, lane + 128, -lane).astype(jnp.float32)

    for part in range(2):
        mine = slice(part * BLK, (part + 1) * BLK)
        acc_ref[mine, :] = jnp.zeros((BLK, BLK), jnp.float32)

        @pl.loop(0, half // 8)
        def _(i):
            tile = perm_ref[pl.ds(pl.multiple_of(part * half + i * 8, 8), 8), :]
            high = tile >> 8
            low = tile & 255
            for first in range(0, 8, step):
                left, right = [], []
                for k in range(first, first + step):
                    value = code * power_ref[i * 8 + k]
                    left.append(
                        jnp.where(rows == high[k:k + 1, :], value, 0.0).astype(jnp.bfloat16)
                    )
                    right.append(
                        jnp.where(rows == low[k:k + 1, :], 1.0, 0.0).astype(jnp.bfloat16)
                    )
                acc_ref[mine, :] += dot_nt(
                    jnp.concatenate(left, axis=1), jnp.concatenate(right, axis=1)
                )

    for r in range(0, BLK, 32):
        late = acc_ref[BLK + r:BLK + r + 32, :]
        held = acc_ref[r:r + 32, :] + late
        size = jnp.abs(held)
        number = jnp.where(late != 0.0, 32768.0, 0.0) + jnp.where(held < 0.0, 128.0, 0.0)
        for bit in (64, 32, 16, 8, 4, 2, 1):
            above = size >= 2.0 ** (bit - 57)
            size = jnp.where(above, size * 2.0 ** -bit, size)
            number = number + jnp.where(above, bit * 256.0, 0.0)
        acc_ref[r:r + 32, :] = number + (size * 2.0 ** 64 - 128.0)

    per_rep = 8 // reps
    for d in range(blocks // 8):
        tile = acc_ref[d * 8:(d + 1) * 8, :]
        for b in range(reps):
            start = BLK + b * (blocks // reps) + d * per_rep
            acc_ref[start:start + per_rep, :] = tile[b * per_rep:(b + 1) * per_rep, :]
    for k in range(2):
        out_ref[k * BLK:(k + 1) * BLK, :] = perm_ref[k * half:(k + 1) * half, :].T
        back_ref[k * BLK:(k + 1) * BLK, :] = acc_ref[
            BLK + k * half:BLK + (k + 1) * half, :
        ].T.astype(jnp.int32)


def index_streams(perm, reps):
    blocks = perm.shape[0] // BLK
    streams = jax.ShapeDtypeStruct((2 * BLK, blocks // 2), jnp.int32)
    powers = jnp.asarray([2.0 ** (k - 64) for k in range(blocks // 2)], jnp.float32)
    out, back = pl.pallas_call(
        functools.partial(inverse_kernel, reps),
        out_shape=(streams, streams),
        in_specs=[WHOLE, SCALARS],
        out_specs=(WHOLE, WHOLE),
        scratch_shapes=[pltpu.VMEM((2 * BLK, BLK), jnp.float32)],
        compiler_params=pltpu.CompilerParams(vmem_limit_bytes=VMEM_LIMIT),
        cost_estimate=pl.CostEstimate(
            flops=2 * BLK * BLK * blocks * BLK, bytes_accessed=8 * blocks * BLK, transcendentals=0
        ),
    )(perm.reshape(blocks, BLK), powers)
    return out.reshape(-1), back.reshape(-1)


def stream(index_ref, streams, sem, table_ref, rows_refs, work):
    sublane = iota((8, LANES), 0)
    size = streams[0].shape[0]
    half = size // 8
    count = half // 2
    copies = [
        pltpu.make_async_copy(index_ref.at[pl.ds(k * size, size)], held, sem.at[k])
        for k, held in enumerate(streams)
    ]

    def gather(i, rows_ref):
        def tile(held, places):
            value = None
            for t in range(8):
                row = jnp.broadcast_to(table_ref[pl.ds(held[places[t]], 1), :], (8, LANES))
                value = row if value is None else jnp.where(sublane == t, row, value)
            return value

        for part in range(2):
            places = [t * half + 2 * i + part for t in range(8)]
            for k in range(0, len(streams), 2):
                both = jnp.concatenate([tile(held, places) for held in streams[k:k + 2]], axis=0)
                first = part * len(streams) * 8 + k * 8
                rows_ref[first:first + 16, :] = both.astype(jnp.bfloat16)

    def begin():
        for copy in copies:
            copy.start()

    def run():
        for copy in copies:
            copy.wait()
        def gather_pair(i, rows_ref):
            for k in range(2):
                gather(2 * jnp.minimum(i, count // 2 - 1) + k, rows_ref.at[pl.ds(k * SPAN, SPAN), :])

        gather_pair(0, rows_refs[0])

        @pl.loop(0, count // 4)
        def _(j):
            for s in range(2):
                i = j * 2 + s
                gather_pair(i + 1, rows_refs[(s + 1) % 2])
                work(i, rows_refs[s % 2])

    return begin, run


def blocks_of(i, blocks):
    return [2 * i, 2 * i + blocks // 2, 2 * i + 1, 2 * i + 1 + blocks // 2]


def surface_kernel(
    arrived_ref, perm_ref, back_ref, pot_ref, surf_ref, out_ref,
    x_ref, x_sem, table_ref, packed_ref, even_ref, odd_ref, *rest
):
    streams, sem = rest[:-1], rest[-1]
    arrival = pltpu.make_async_copy(arrived_ref, x_ref, x_sem)
    arrival.start()
    pieces, vecs, width = x_ref.shape
    points = table_ref.shape[0]
    per_group = pieces // GROUPS
    group_rows = points // GROUPS
    row, column = iota((LANES, GROUPS * LANES), 0), iota((LANES, GROUPS * LANES), 1)
    fold = jnp.where(
        (row // PAD == column // LANES) & (row % PAD == column % PAD), 1.0, 0.0
    ).astype(jnp.bfloat16)
    unit = jnp.where(iota((BLK, BLK), 0) == iota((BLK, BLK), 1), 1.0, 0.0).astype(jnp.bfloat16)
    lane_group = iota((BLK, LANES), 1) // PAD
    count = points // SPAN
    blocks = points // BLK

    def folded(rows_ref, k):
        wide = jnp.concatenate([
            rows_ref[k * SPAN + q * BLK:k * SPAN + (q + 1) * BLK, :] for q in range(GROUPS)
        ], axis=1)
        return dot_nt(fold, wide).astype(jnp.bfloat16)

    def spread(rows, starts):
        for q in range(GROUPS):
            table_ref[pl.ds(pl.multiple_of(starts[q], BLK), BLK), :] = jnp.where(
                lane_group == q, rows, 0.0
            )

    def to_grid_and_back(i, rows_ref):
        values = jnp.concatenate([folded(rows_ref, k) for k in range(2)], axis=0)
        projected = jnp.dot(values, surf_ref[...], preferred_element_type=jnp.float32)
        held = blocks_of(2 * i, blocks) + blocks_of(2 * i + 1, blocks)
        weighted = jnp.concatenate([
            projected[q * PAD:(q + 1) * PAD] * pot_ref[pl.ds(block, 1), :]
            for q, block in enumerate(held)
        ], axis=0).astype(jnp.bfloat16)
        returned = dot_nt(surf_ref[...], weighted).astype(jnp.bfloat16).astype(jnp.float32)
        for k in range(2):
            start = pl.multiple_of((2 * i + k) * BLK, BLK)
            packed_ref[pl.ds(start, BLK), :] = returned[:, k * LANES:(k + 1) * LANES]

    def to_basis(i, rows_ref):
        per_piece = out_ref.shape[2] // BLK
        for k in range(2):
            values = folded(rows_ref, k)
            for q in range(GROUPS):
                at = (q // per_piece) * BLK
                piece = 2 * i + k + (q % per_piece) * (out_ref.shape[0] // per_piece)
                out_ref[piece, :, at:at + BLK] = values[q * PAD:q * PAD + vecs]

    begin, run = stream(perm_ref, streams, sem, table_ref, (even_ref, odd_ref), to_grid_and_back)
    begin()
    arrival.wait()
    chunk = 512

    @pl.loop(0, per_group)
    def _(d):
        for c in range(0, width, chunk):
            parts = []
            for q in range(GROUPS):
                parts.append(x_ref[q * per_group + d, :, c:c + chunk].astype(jnp.float32))
                parts.append(jnp.zeros((PAD - vecs, chunk), jnp.float32))
            stacked = jnp.concatenate(parts, axis=0).astype(jnp.bfloat16)
            for h in range(0, chunk, BLK):
                rows = dot_nt(unit, stacked[:, h:h + BLK])
                spread(rows, [q * group_rows + d * width + c + h for q in range(GROUPS)])

    run()
    begin, run = stream(back_ref, streams, sem, table_ref, (even_ref, odd_ref), to_basis)
    begin()

    @pl.loop(0, count)
    def _(i):
        rows = packed_ref[pl.ds(pl.multiple_of(i * BLK, BLK), BLK), :]
        spread(rows, [block * BLK for block in blocks_of(i, blocks)])

    run()


def surface_pass(arrived, perm, back, potential, surface, reps):
    pieces, vecs, width = arrived.shape
    points = perm.shape[0]
    return pl.pallas_call(
        surface_kernel,
        out_shape=jax.ShapeDtypeStruct((pieces * reps, vecs, width // reps), jnp.bfloat16),
        in_specs=[pl.BlockSpec(memory_space=pl.ANY)] + [WHOLE] * 4,
        out_specs=WHOLE,
        scratch_shapes=[
            pltpu.VMEM(arrived.shape, jnp.bfloat16),
            pltpu.SemaphoreType.DMA,
            pltpu.VMEM((points, LANES), jnp.float32),
            pltpu.VMEM((points // GROUPS, LANES), jnp.float32),
            pltpu.VMEM((2 * SPAN, LANES), jnp.bfloat16),
            pltpu.VMEM((2 * SPAN, LANES), jnp.bfloat16),
        ] + [pltpu.SMEM((4 * BLK,), jnp.int32)] * 64 + [pltpu.SemaphoreType.DMA((64,))],
        compiler_params=pltpu.CompilerParams(vmem_limit_bytes=VMEM_LIMIT),
        cost_estimate=pl.CostEstimate(
            flops=4 * vecs * points * BLK, bytes_accessed=300_000_000, transcendentals=0
        ),
    )(arrived, perm, back, potential.reshape(-1, BLK), surface)


def source_kernel(vecs_ref, low_ref, high_ref, column_ref, weight_ref, out_ref, wide_ref):
    reps = out_ref.shape[0]
    edge = low_ref.shape[1]
    rows = vecs_ref.shape[1]
    blocks = rows // BLK
    piece_blocks = out_ref.shape[3] * reps // (blocks * BLK)
    wide_ref[:, 0:edge] = low_ref[...]
    wide_ref[:, edge + rows:] = high_ref[...]
    per_piece = 8
    per_rep = per_piece // reps

    @pl.loop(0, blocks // per_piece)
    def _(j):
        start = pl.multiple_of(j * per_piece * BLK, per_piece * BLK)
        wide_ref[:, pl.ds(edge + start, per_piece * BLK)] = vecs_ref[:, pl.ds(start, per_piece * BLK)]

    @pl.loop(0, blocks // per_piece)
    def _(j):
        for k in range(per_piece):
            a = j * per_piece + k
            total = None
            for m in range(COUPLINGS_PER_ROW):
                c = a * COUPLINGS_PER_ROW + m
                at = pl.multiple_of(column_ref[c] * BLK, BLK)
                term = wide_ref[:, pl.ds(at, BLK)].astype(jnp.float32) * weight_ref[c]
                total = term if total is None else total + term
            to = pl.ds(pl.multiple_of(j * per_rep * BLK, per_rep * BLK) + (k % per_rep) * BLK, BLK)
            here = pl.multiple_of(a * BLK, BLK)
            out_ref[k // per_rep, 0, :, to] = vecs_ref[:, pl.ds(here, BLK)]
            out_ref[k // per_rep, 1, :, to] = total.astype(jnp.bfloat16)


def source_of(basis_vecs, low, high, columns, weights, reps):
    vecs, rows = basis_vecs.shape
    return pl.pallas_call(
        source_kernel,
        out_shape=jax.ShapeDtypeStruct((reps, 2, vecs, rows // reps), jnp.bfloat16),
        in_specs=[WHOLE, WHOLE, WHOLE, SCALARS, SCALARS],
        out_specs=WHOLE,
        scratch_shapes=[pltpu.VMEM((vecs, rows + 2 * low.shape[1]), jnp.bfloat16)],
        compiler_params=pltpu.CompilerParams(vmem_limit_bytes=VMEM_LIMIT),
        cost_estimate=pl.CostEstimate(
            flops=6 * vecs * rows, bytes_accessed=12 * vecs * rows, transcendentals=0
        ),
    )(basis_vecs, low, high, columns, weights)


def vector_kernel(
    moved_ref, kinetic_ref, precond_ref, vectors_ref, kin_ref, sums_ref, total_ref
):
    step = pl.program_id(0)
    reps, _, vecs, width = moved_ref.shape
    count = reps * vecs

    @pl.when(step == 0)
    def _():
        total_ref[...] = jnp.zeros_like(total_ref)

    def ordered(k):
        return jnp.concatenate([moved_ref[b, k].astype(jnp.float32) for b in range(reps)], axis=0)

    vectors = ordered(0)
    vectors_16 = vectors.astype(jnp.bfloat16)
    vectors_ref[...] = vectors_16
    scale = precond_ref[...]
    left = jnp.concatenate(three_parts(vectors * (scale * scale)), axis=0)
    total_ref[...] += dot_nt(left, vectors_16)
    source = ordered(1).astype(jnp.bfloat16)
    blocks = [source[:, h:h + BLK] for h in range(0, width, BLK)]
    kin = jnp.dot(jnp.concatenate(blocks, axis=0), kinetic_ref[...], preferred_element_type=jnp.float32)
    for h in range(width // BLK):
        kin_ref[:, h * BLK:(h + 1) * BLK] = kin[h * count:(h + 1) * count]

    @pl.when(step == pl.num_programs(0) - 1)
    def _():
        sums_ref[...] = (
            total_ref[0:count] + total_ref[count:2 * count] + total_ref[2 * count:3 * count]
        )


def vectors_of(moved, kinetic, precond, steps):
    reps, _, vecs, rows = moved.shape
    width = rows // steps
    count = reps * vecs
    return pl.pallas_call(
        vector_kernel,
        grid=(steps,),
        out_shape=(
            jax.ShapeDtypeStruct((count, rows), jnp.bfloat16),
            jax.ShapeDtypeStruct((count, rows), jnp.float32),
            jax.ShapeDtypeStruct((count, count), jnp.float32),
        ),
        in_specs=[
            pl.BlockSpec((reps, 2, vecs, width), lambda i: (0, 0, 0, i)),
            pl.BlockSpec((BLK, BLK), lambda i: (0, 0)),
            pl.BlockSpec((1, width), lambda i: (0, i)),
        ],
        out_specs=(
            pl.BlockSpec((count, width), lambda i: (0, i)),
            pl.BlockSpec((count, width), lambda i: (0, i)),
            pl.BlockSpec((count, count), lambda i: (0, 0)),
        ),
        scratch_shapes=[pltpu.VMEM((3 * count, count), jnp.float32)],
        compiler_params=pltpu.CompilerParams(vmem_limit_bytes=VMEM_LIMIT),
        cost_estimate=pl.CostEstimate(
            flops=12 * count * count * rows, bytes_accessed=8 * count * rows, transcendentals=0
        ),
    )(moved, kinetic, precond)


def image_kernel(
    core_ref, vectors_ref, kin_ref, vector_sums_ref, pot_ref, precond_ref,
    image_ref, keep_ref, give_ref, total_ref, sums_ref
):
    step = pl.program_id(0)
    count, width = vectors_ref.shape
    reps, _, vecs, segment = pot_ref.shape

    @pl.when(step == 0)
    def _():
        total_ref[...] = jnp.zeros_like(total_ref)

    for s in range(width // segment):
        at = slice(s * segment, (s + 1) * segment)
        pot = jnp.concatenate([pot_ref[b, s].astype(jnp.float32) for b in range(reps)], axis=0)
        image = (kin_ref[:, at] + pot).astype(jnp.bfloat16)
        image_ref[:, at] = image
        scale = precond_ref[0:1, at]
        scaled = three_parts(image.astype(jnp.float32) * (scale * scale))
        left = jnp.concatenate(scaled + [image], axis=0)
        total_ref[...] += dot_nt(left, jnp.concatenate([image, vectors_ref[:, at]], axis=0))

    @pl.when(step == pl.num_programs(0) - 1)
    def _():
        scaled = total_ref[0:count] + total_ref[count:2 * count] + total_ref[2 * count:3 * count]
        own, cross = scaled[:, 0:count], scaled[:, count:2 * count]
        plain = total_ref[3 * count:4 * count, count:2 * count]
        vector = vector_sums_ref[...]
        row, column = iota((count, count), 0), iota((count, count), 1)
        own = jnp.where(row <= column, own, vector)
        diagonal = jnp.sum(jnp.where(row == column, vector, 0.0), axis=0, keepdims=True)
        sums_ref[0:count, :] = jnp.concatenate([own, cross[:, 0:PAD]], axis=1)
        sums_ref[count:2 * count, :] = jnp.concatenate([plain, cross[:, PAD:2 * PAD]], axis=1)
        sums_ref[2 * count:2 * count + vecs, :] = jnp.concatenate(
            [cross[b * vecs:(b + 1) * vecs, 2 * PAD:3 * PAD] for b in range(reps)], axis=1
        )
        sums_ref[2 * count + vecs:, :] = jnp.broadcast_to(
            jnp.concatenate([diagonal, jnp.zeros((1, PAD), jnp.float32)], axis=1), (8, LANES)
        )
        size = keep_ref.shape[0]
        core = core_ref[0]
        keep_ref[...] = sums_ref[pl.ds(pl.multiple_of(core * size, 8), size), :]
        give_ref[...] = sums_ref[pl.ds(pl.multiple_of((1 - core) * size, 8), size), :]


def image_of(core, vectors, kin, vector_sums, pot, precond, steps):
    count, rows = vectors.shape
    reps, pieces, vecs, segment = pot.shape
    width = rows // steps
    packed = (2 * count + vecs + 8, LANES)
    half = (packed[0] // 2, LANES)
    return pl.pallas_call(
        image_kernel,
        grid=(steps,),
        out_shape=(
            jax.ShapeDtypeStruct((count, rows), jnp.bfloat16),
            jax.ShapeDtypeStruct(half, jnp.float32),
            jax.ShapeDtypeStruct(half, jnp.float32),
        ),
        in_specs=[
            SCALARS,
            pl.BlockSpec((count, width), lambda i: (0, i)),
            pl.BlockSpec((count, width), lambda i: (0, i)),
            pl.BlockSpec((count, count), lambda i: (0, 0)),
            pl.BlockSpec((reps, pieces // steps, vecs, segment), lambda i: (0, i, 0, 0)),
            pl.BlockSpec((1, width), lambda i: (0, i)),
        ],
        out_specs=(
            pl.BlockSpec((count, width), lambda i: (0, i)),
            pl.BlockSpec(half, lambda i: (0, 0)),
            pl.BlockSpec(half, lambda i: (0, 0)),
        ),
        scratch_shapes=[
            pltpu.VMEM((4 * count, 2 * count), jnp.float32),
            pltpu.VMEM(packed, jnp.float32),
        ],
        compiler_params=pltpu.CompilerParams(vmem_limit_bytes=VMEM_LIMIT),
        cost_estimate=pl.CostEstimate(
            flops=16 * count * count * rows, bytes_accessed=10 * count * rows, transcendentals=0
        ),
    )(core, vectors, kin, vector_sums, pot, precond)


def solve_kernel(
    full_rows, reps, core_ref, mine_ref, other_ref, vectors_ref, image_ref, precond_ref,
    out_ref, rayleigh_ref, mix_ref, sums_ref
):
    count, width = image_ref.shape
    vecs = count // reps

    @pl.when(pl.program_id(0) == 0)
    def _():
        size = mine_ref.shape[0]
        core = core_ref[0]
        sums_ref[pl.ds(pl.multiple_of(core * size, 8), size), :] = mine_ref[...]
        sums_ref[pl.ds(pl.multiple_of((1 - core) * size, 8), size), :] = other_ref[...]
        row, column = iota((count, count), 0), iota((count, count), 1)
        shared = sums_ref[0:count, 0:count]
        shared_t = shared.T
        own = jnp.where(row <= column, shared, shared_t)
        vector = jnp.where(row <= column, shared_t, shared)
        diagonal = sums_ref[2 * count + vecs:2 * count + vecs + 1, 0:count]
        vector = jnp.where(row == column, diagonal, vector)
        turned = sums_ref[count:2 * count, 0:count] / full_rows
        rayleigh = turned.T
        rayleigh_ref[...] = rayleigh
        third = jnp.concatenate([
            sums_ref[2 * count:2 * count + vecs, b * PAD:(b + 1) * PAD] for b in range(reps)
        ], axis=0)
        mixed = jnp.concatenate(
            [sums_ref[0:count, count:], sums_ref[count:2 * count, count:], third], axis=1
        )
        cross = dot_exact(mixed, rayleigh)
        last = dot_exact(turned, dot_exact(vector, rayleigh))
        gram = (own - cross - cross.T + last) / full_rows
        pad = jnp.zeros((8, LANES - count), jnp.float32)
        row, column = iota((8, LANES), 0), iota((8, LANES), 1)
        left, right = [], []
        for k in range(0, count, 8):
            left.append(jnp.concatenate([gram[k:k + 8, :], pad], axis=1))
            right.append(jnp.where(row + k == column, 1.0, 0.0))
        for j in range(count):
            own, at = j // 8, j % 8
            over = 1.0 / left[own][at:at + 1, j:j + 1]
            pivot_left = left[own][at:at + 1, :] * over
            pivot_right = right[own][at:at + 1, :] * over
            for k in range(own, count // 8):
                ratio = left[k][:, j:j + 1]
                if k == own:
                    ratio = jnp.where(row[:, 0:1] > at, ratio, 0.0)
                left[k] = left[k] - ratio * pivot_left
                right[k] = right[k] - ratio * pivot_right
        scaled = []
        for k in range(count // 8):
            pivots = jnp.where(row + k * 8 == column, left[k], 0.0)
            scaled.append(right[k] * lax.rsqrt(jnp.sum(pivots, axis=1, keepdims=True)))
        inverse = jnp.concatenate(scaled, axis=0)[:, 0:count]
        parts = three_parts(inverse) + three_parts(-dot_exact(inverse, turned))
        for k in range(3):
            mix_ref[k * count:(k + 1) * count, 0:count] = parts[k]
            mix_ref[k * count:(k + 1) * count, count:2 * count] = parts[3 + k]

    both = jnp.concatenate([image_ref[...], vectors_ref[...]], axis=0)
    chunk = 512
    for s in range(0, width, chunk):
        parts = jnp.dot(mix_ref[...], both[:, s:s + chunk], preferred_element_type=jnp.float32)
        total = (parts[2 * count:] + parts[count:2 * count]) + parts[0:count]
        out_ref[:, 0, s:s + chunk] = total * precond_ref[0:1, s:s + chunk]


def solved_of(core, mine, other, vectors, image, precond, full_rows, reps, steps):
    count, rows = image.shape
    width = rows // steps
    return pl.pallas_call(
        functools.partial(solve_kernel, full_rows, reps),
        grid=(steps,),
        out_shape=(
            jax.ShapeDtypeStruct((count, 1, rows), jnp.float32),
            jax.ShapeDtypeStruct((count, count), jnp.float32),
        ),
        in_specs=[
            SCALARS,
            pl.BlockSpec(mine.shape, lambda i: (0, 0)),
            pl.BlockSpec(mine.shape, lambda i: (0, 0)),
            pl.BlockSpec((count, width), lambda i: (0, i)),
            pl.BlockSpec((count, width), lambda i: (0, i)),
            pl.BlockSpec((1, width), lambda i: (0, i)),
        ],
        out_specs=(
            pl.BlockSpec((count, 1, width), lambda i: (0, 0, i)),
            pl.BlockSpec((count, count), lambda i: (0, 0)),
        ),
        scratch_shapes=[
            pltpu.VMEM((3 * count, 2 * count), jnp.bfloat16),
            pltpu.VMEM((2 * mine.shape[0], LANES), jnp.float32),
        ],
        compiler_params=pltpu.CompilerParams(vmem_limit_bytes=VMEM_LIMIT),
        cost_estimate=pl.CostEstimate(
            flops=12 * count * count * rows, bytes_accessed=8 * count * rows, transcendentals=0
        ),
    )(core, mine, other, vectors, image, precond)


def sum_over_devices(keep, give):
    def turned(x, axis, stride, shift):
        pairs = []
        for i in range(lax.axis_size(axis)):
            digit = (i // stride) % 4
            pairs.append((i, i + ((digit + shift) % 4 - digit) * stride))
        return lax.ppermute(x, axis, pairs)

    swap = [(i, i ^ 1) for i in range(lax.axis_size("row"))]
    x = keep + lax.ppermute(give, "row", swap)
    for axis, stride in (("rep", 1), ("row", 8), ("row", 2)):
        up, down, across = (turned(x, axis, stride, shift) for shift in (1, 3, 2))
        x = (x + across) + (up + down)
    return x, lax.ppermute(x, "row", swap)


def body(
    basis_vecs, potential, surface, grid_perm, kinetic, couplings, coupling_coefficient, precond
):
    vecs, rows = basis_vecs.shape
    pieces = lax.axis_size("row")
    reps = lax.axis_size("rep")
    width = rows // pieces
    blocks = rows // BLK
    edge = HB * BLK
    forward = [(i, i + 1) for i in range(pieces - 1)]
    backward = [(i + 1, i) for i in range(pieces - 1)]
    low = lax.ppermute(basis_vecs[:, rows - edge:], "row", forward)
    high = lax.ppermute(basis_vecs[:, :edge], "row", backward)
    by_piece = basis_vecs.reshape(vecs, pieces, width).transpose(1, 0, 2)
    arrived = lax.all_to_all(by_piece, "row", split_axis=0, concat_axis=0, tiled=True)
    columns = couplings[:, 1] - (lax.axis_index("row") * blocks - HB)
    by_rep = source_of(basis_vecs, low, high, columns, coupling_coefficient, reps)
    out, back = index_streams(grid_perm, reps)
    by_rep, out, back = lax.optimization_barrier((by_rep, out, back))
    moved = lax.all_to_all(by_rep, "rep", split_axis=0, concat_axis=0, tiled=True)
    restored = surface_pass(arrived, out, back, potential, surface, reps)
    restored, moved = lax.optimization_barrier((restored, moved))
    pot = lax.all_to_all(restored, ("rep", "row"), split_axis=0, concat_axis=0, tiled=True)
    pot = pot.reshape(reps, pieces, vecs, width // reps)
    scale = precond.reshape(1, -1)
    core = (lax.axis_index("row") % 2).reshape(1)
    vectors, kin, vector_sums = vectors_of(moved, kinetic, scale, 4)
    image, keep, give = image_of(core, vectors, kin, vector_sums, pot, scale, 2)
    mine, other = sum_over_devices(keep, give)
    solved, rayleigh = solved_of(
        core, mine, other, vectors, image, scale, float(rows * pieces), reps, 2
    )
    return (solved.reshape(reps * vecs, 1, 1, -1), rayleigh)


def solution(mesh):
    in_specs = (
        P("rep", "row"),
        P("row"),
        P(),
        P("row"),
        P(),
        P("row", None),
        P("row"),
        P("row", "rep", None),
    )
    out_specs = (P(None, "row", "rep", None), P())
    return jax.shard_map(body, mesh=mesh, in_specs=in_specs, out_specs=out_specs, check_vma=False)
```
